512 devices in a mesh: harm: 64 (over y, z), grp: 8 (over x, core).
Axes of the slice: x: 4, y: 4, z: 16, core: 2. Of those that a mesh axis runs over, the one named last changes fastest.
Arguments:
- vectors: float32 [128, 16, 65536], P('harm', None, 'grp'), may hold values from -6 to 6
- stiffness: float32 [65536], P('grp'), may hold values from 0.5 to 4
- attach: int32 [8192], P('grp'), may hold values from 0 to 8191, as said below
- live: int32 [8], P('grp'), may hold values from 512 to 1024
- pair_harm: int32 [64], replicated, may hold values from 0 to 63, each once
- mistune: float32 [128, 8, 1024], P(None, 'grp'), may hold values from 0.5 to 2
Outputs:
- image: float32 [128, 16, 65536], P('harm', None, 'grp')
- gram: float32 [2, 16, 16], replicated
The draws below stay inside these ranges and needn't reach their ends.
Inputs may be any that keep to these rules, and one draw needn't show every extreme that they name: `attach`: within each block of 1024 rows of one grp index the entries are distinct.
All inputs are finite; a program needn't handle non-finite values.
Results may differ from the reference program's by a relative error of at most 0.00005.
Values sent between devices are 32-bit elements; how exact they have to be, the bound alone decides.
No kernel may reach another device: no remote copies, remote signals or barrier semaphores. Data moves between devices by JAX's collectives and lax.ppermute only.
A program may use at most 64 MiB of HBM per device.

```python
import math
import jax
import jax.numpy as jnp
from jax import lax

BLADES = 128
VECS = 16
SEC_DEV = 8192
R_DEV = 1024
HALF = 64
SECTOR = 65536
ROWS = 8192
N_GRP = 8


def draw_attach(key, part):
    key = jax.random.fold_in(key, 7)
    keys = jax.random.split(key, ROWS // R_DEV)
    picks = jax.vmap(lambda k: jax.random.permutation(k, SEC_DEV)[:R_DEV])(keys)
    return picks.reshape(ROWS).astype(jnp.int32)


def set_ends(result, rng, smallest, top_value):
    shape = result.shape
    index_at = [jax.random.randint(jax.random.fold_in(rng, axis), (), 0, shape[axis]) for axis in range(len(shape))]
    result = result.at[tuple(index_at)].set(smallest)
    longest = shape.index(max(shape))
    index_at[longest] = (index_at[longest] + 1) % shape[longest]
    return result.at[tuple(index_at)].set(top_value)


def steps_of(key, dims, shards, smallest, high):
    def one(position, shards_of):
        draws = jax.random.uniform(jax.random.fold_in(jax.random.fold_in(key, 6), position), (shards_of,), jnp.float32, smallest / len(shards), high / len(shards))
        return jnp.repeat(jnp.exp(draws), dims[position] // shards_of).reshape((-1,) + (1,) * (len(dims) - position - 1))

    loudness = one(*shards[0])
    for cut in shards[1:]:
        loudness = loudness * one(*cut)
    return loudness


def scatter_about(key, shape, scale, reach, cuts=(), kind=jnp.bfloat16):
    values = jax.random.normal(key, shape, jnp.float32) * scale
    if len(cuts) > 0:
        values = steps_of(key, shape, cuts, -0.22, 0.18) * values
    return jnp.clip(values, min=-reach, max=reach).astype(kind)


def setup_inputs(seed: int = 0) -> dict:
    key_list = jax.random.split(jax.random.key(seed), 7)
    return {
        "vectors": scatter_about(key_list[0], (BLADES, VECS, SECTOR), 1.0, 6.0, ((0, 64), (2, 8)), jnp.float32),
        "stiffness": jnp.clip(jnp.exp(math.log(4.0) - 2.0794415 * jax.random.uniform(key_list[1], (SECTOR,), jnp.float32) ** steps_of(key_list[1], (SECTOR,), ((0, 8),), -0.2, 0.2)), 0.5, 4.0),
        "attach": draw_attach(jax.random.fold_in(key_list[6], 71), 0),
        "live": set_ends(jax.random.randint(key_list[3], (N_GRP,), R_DEV // 2, R_DEV + 1), jax.random.fold_in(key_list[3], 1), R_DEV // 2, R_DEV).astype(jnp.int32),
        "pair_harm": jax.random.permutation(key_list[4], HALF).astype(jnp.int32),
        "mistune": jnp.clip(jnp.exp(math.log(2.0) - 1.3862944 * jax.random.uniform(key_list[5], (BLADES, N_GRP, R_DEV), jnp.float32) ** steps_of(key_list[5], (BLADES, N_GRP, R_DEV), ((1, 8),), -0.2, 0.2)), 0.5, 2.0),
    }


def slot_tables(pair_harm, slots, blades):
    half = blades // 2
    onehot = (slots % half)[:, None] == jnp.arange(half, dtype=jnp.int32)[None, :]
    harmonic = lax.optimization_barrier(jnp.sum(jnp.where(onehot, pair_harm[None, :], 0), axis=1)).astype(jnp.int32)
    imag = slots >= half
    theta = jnp.where(harmonic == 0, jnp.where(imag, math.pi, 0.0), 2.0 * math.pi * harmonic.astype(jnp.float32) / blades).astype(jnp.float32)
    coup = jnp.where(harmonic == 0, 0.0, jnp.where(imag, -1.0, 1.0) * jnp.sin(theta)).astype(jnp.float32)
    return (theta, coup, harmonic, imag)

def basis_table(theta, harmonic, imag, blades):
    blade_ids = jnp.arange(blades, dtype=jnp.float32)
    angle = blade_ids[:, None] * theta[None, :]
    wide = math.sqrt(2.0 / blades) * jnp.where(imag[None, :], jnp.sin(angle), jnp.cos(angle))
    return jnp.where(harmonic[None, :] == 0, jnp.cos(angle) / math.sqrt(blades), wide).astype(jnp.float32)

def reference(vectors, stiffness, attach, live, pair_harm, mistune):
    slots = jnp.arange(BLADES, dtype=jnp.int32)
    theta, coup, harmonic, imag = slot_tables(pair_harm, slots, BLADES)
    basis = basis_table(theta, harmonic, imag, BLADES)
    padded = jnp.pad(vectors, ((0, 0), (0, 0), (1, 1)))
    lower = padded[:, :, :-2]
    upper = padded[:, :, 2:]
    partner = jnp.roll(padded, -HALF, axis=0)
    diag = 2.0 + stiffness[None, None, :] + 2.0 * (1.0 - jnp.cos(theta))[:, None, None]
    adjusted = diag * vectors - lower - upper + coup[:, None, None] * (partner[:, :, 2:] - partner[:, :, :-2])
    row_ids = jnp.arange(ROWS, dtype=jnp.int32)
    owner = row_ids // R_DEV
    columns = (owner * SEC_DEV + attach).astype(jnp.int32)
    alive = (row_ids % R_DEV < live[owner]).astype(jnp.float32)
    rows = vectors[:, :, columns] * alive[None, None, :]
    blade = jnp.einsum('bk,kvr->bvr', basis, rows, precision=lax.Precision.HIGHEST)
    forced = mistune.reshape(BLADES, ROWS)[:, None, :] * blade
    back = jnp.einsum('bk,bvr->kvr', basis, forced, precision=lax.Precision.HIGHEST) * alive[None, None, :]
    image = adjusted.at[:, :, columns].add(back)
    first = jnp.einsum('kvs,kws->vw', vectors, image, precision=lax.Precision.HIGHEST)
    second = jnp.einsum('kvs,kws->vw', image, image, precision=lax.Precision.HIGHEST)
    return (image, jnp.stack([first, second]))
```

```python
import math

import jax
import jax.numpy as jnp
from jax import lax
from jax.experimental import pallas as pl
from jax.experimental.pallas import tpu as pltpu
from jax.sharding import PartitionSpec as P

LANES = 128
OCT = 8
PIECE = 16


def slot_tables(pair_harm, slots, blades):
    half = blades // 2
    onehot = (slots % half)[:, None] == jnp.arange(half, dtype=jnp.int32)[None, :]
    harmonic = jnp.sum(jnp.where(onehot, pair_harm[None, :], 0), axis=1)
    imag = slots >= half
    theta = jnp.where(
        harmonic == 0,
        jnp.where(imag, math.pi, 0.0),
        2.0 * math.pi * harmonic.astype(jnp.float32) / blades,
    )
    coup = jnp.where(harmonic == 0, 0.0, jnp.where(imag, -1.0, 1.0) * jnp.sin(theta))
    return (theta, coup, harmonic, imag)


def basis_table(theta, harmonic, imag, blades):
    blade_ids = jnp.arange(blades, dtype=jnp.float32)
    angle = blade_ids[:, None] * theta[None, :]
    wide = math.sqrt(2.0 / blades) * jnp.where(imag[None, :], jnp.sin(angle), jnp.cos(angle))
    return jnp.where(harmonic[None, :] == 0, jnp.cos(angle) / math.sqrt(blades), wide)


def iota(shape, dim):
    return lax.broadcasted_iota(jnp.int32, shape, dim)


def pick(tile, index):
    return jnp.take_along_axis(tile, index, axis=1, mode="promise_in_bounds")


def swap_blocks(tile):
    sub = iota(tile.shape, 0)
    block = iota(tile.shape, 1) // PIECE
    for bit in (1, 2, 4):
        from_low = pltpu.roll(pltpu.roll(tile, bit, 0), LANES - PIECE * bit, 1)
        from_high = pltpu.roll(pltpu.roll(tile, OCT - bit, 0), PIECE * bit, 1)
        s, b = (sub & bit) != 0, (block & bit) != 0
        tile = jnp.where(s & ~b, from_low, jnp.where(~s & b, from_high, tile))
    return tile


def gather_kernel(attach_ref, v_ref, out_ref):
    chunks, tiles = attach_ref.shape[0], v_ref.shape[2] // LANES
    low, high = [], []
    for c in range(chunks):
        col = jnp.broadcast_to(attach_ref[c : c + 1, :], (OCT, LANES))
        low.append(col & (LANES - 1))
        high.append(col >> 7)

    def step(i, accs):
        at = pl.ds(pl.multiple_of(i * LANES, LANES), LANES)
        tile = [v_ref[j // 2, OCT * (j % 2) : OCT * (j % 2) + OCT, at] for j in range(4)]
        new = []
        for c in range(chunks):
            here = high[c] == i
            for j in range(4):
                new.append(jnp.where(here, pick(tile[j], low[c]), accs[4 * c + j]))
        return tuple(new)

    zero = jnp.zeros((OCT, LANES), jnp.float32)
    accs = lax.fori_loop(0, tiles, step, (zero,) * (4 * chunks))
    for c in range(chunks):
        for j in range(4):
            out_ref[pl.ds(4 * OCT * c + j, OCT, stride=4), :] = swap_blocks(accs[4 * c + j])


def blade_kernel(where_ref, recv_ref, mistune_ref, basis_ref, basis_t_ref, out_ref):
    me, live = where_ref[0], where_ref[1]
    owners = recv_ref.shape[0] // 4
    part = [recv_ref[pl.ds(j, owners, stride=4), :] for j in range(4)]
    rows = jnp.concatenate(
        [jnp.concatenate([part[0], part[1]], axis=1), jnp.concatenate([part[2], part[3]], axis=1)], axis=0
    )
    blades = rows.shape[0]
    lane = iota((1, 2 * LANES), 1)
    alive = me * PIECE + (lane & (PIECE - 1)) < live
    rows = jnp.where(alive, rows, 0.0)
    blade = jnp.dot(basis_ref[...], rows, precision=lax.Precision.HIGHEST, preferred_element_type=jnp.float32)
    chunk = mistune_ref[pl.ds(me // OCT, blades, stride=OCT), :]
    index = (me % OCT) * PIECE + (iota((blades, LANES), 1) & (PIECE - 1))
    stiff = pick(chunk, index)
    forced = jnp.concatenate([stiff, stiff], axis=1) * blade
    back = jnp.dot(basis_t_ref[...], forced, precision=lax.Precision.HIGHEST, preferred_element_type=jnp.float32)
    back = jnp.where(alive, back, 0.0)
    for j in range(4):
        k2, vh = j // 2, j % 2
        out_ref[pl.ds(j, owners, stride=4), :] = back[owners * k2 : owners * (k2 + 1), LANES * vh : LANES * (vh + 1)]


def split3(x):
    a = x.astype(jnp.bfloat16)
    rest = x - a.astype(jnp.float32)
    b = rest.astype(jnp.bfloat16)
    return [a, b, (rest - b.astype(jnp.float32)).astype(jnp.bfloat16)]


def final_kernel(coef_ref, attach_ref, stiff_ref, v_ref, p_ref, recv_ref, image_ref, gram_ref, inv_ref, back_ref):
    tiles = stiff_ref.shape[0]
    rows = attach_ref.shape[1]
    chunks = rows // LANES
    attach = attach_ref[...]
    r = iota((1, rows), 1)
    in_tile = (iota((tiles, rows), 0) == (attach >> 7)).astype(jnp.bfloat16)
    in_lane = iota((LANES, rows), 0) == (attach & (LANES - 1))
    nt = (((1,), (1,)), ((), ()))
    for n, value in enumerate(((r >> 7) + 1, r & (LANES - 1))):
        weighted = jnp.where(in_lane, value.astype(jnp.float32), 0.0).astype(jnp.bfloat16)
        inv_ref[n] = lax.dot_general(in_tile, weighted, nt, preferred_element_type=jnp.float32).astype(jnp.int32)
    for c in range(chunks):
        for j in range(4):
            back_ref[4 * c + j] = swap_blocks(recv_ref[pl.ds(4 * OCT * c + j, OCT, stride=4), :])
    lane = iota((OCT, LANES), 1)
    first, last = lane == 0, lane == LANES - 1
    per = 4

    def step(g, total):
        gram = total
        wide = [[[], []], [[], []]]
        for t in range(per):
            i = g * per + t
            here = pl.ds(pl.multiple_of(i * LANES, LANES), LANES)
            after = pl.ds(pl.multiple_of((i + 1) * LANES, LANES), LANES)
            before = pl.ds(pl.multiple_of(jnp.where(i == 0, tiles, i - 1) * LANES, LANES), LANES)
            stiff = jnp.broadcast_to(stiff_ref[pl.ds(i, 1), :], (OCT, LANES))
            chunk = jnp.broadcast_to(inv_ref[0, pl.ds(i, 1), :], (OCT, LANES))
            index = jnp.broadcast_to(inv_ref[1, pl.ds(i, 1), :], (OCT, LANES))
            for j in range(4):
                k2, o = j // 2, OCT * (j % 2)
                v = v_ref[k2, o : o + OCT, here]
                lo = pltpu.roll(jnp.where(last, v_ref[k2, o : o + OCT, before], v), 1, 1)
                hi = pltpu.roll(jnp.where(first, v_ref[k2, o : o + OCT, after], v), LANES - 1, 1)
                p = p_ref[k2, o : o + OCT, here]
                plo = pltpu.roll(jnp.where(last, p_ref[k2, o : o + OCT, before], p), 1, 1)
                phi = pltpu.roll(jnp.where(first, p_ref[k2, o : o + OCT, after], p), LANES - 1, 1)
                value = (coef_ref[k2] + stiff) * v - lo - hi + coef_ref[2 + k2] * (phi - plo)
                back = jnp.zeros((OCT, LANES), jnp.float32)
                for c in range(chunks):
                    back = jnp.where(chunk == c + 1, pick(back_ref[4 * c + j], index), back)
                value = value + back
                image_ref[k2, o : o + OCT, here] = value
                wide[k2][j % 2].append((v, value))
        for k2 in range(2):
            v = jnp.concatenate([jnp.concatenate([x[0] for x in wide[k2][o]], axis=1) for o in range(2)], axis=0)
            w = jnp.concatenate([jnp.concatenate([x[1] for x in wide[k2][o]], axis=1) for o in range(2)], axis=0)
            left = jnp.concatenate(split3(v) + split3(w), axis=0)
            right = jnp.concatenate(split3(w), axis=0)
            gram = gram + lax.dot_general(left, right, nt, preferred_element_type=jnp.float32)
        return gram

    vecs = image_ref.shape[1]
    total = lax.fori_loop(0, tiles // per, step, jnp.zeros((6 * vecs, 3 * vecs), jnp.float32))
    for n in range(2):
        gram = jnp.zeros((vecs, vecs), jnp.float32)
        for a in range(3):
            for b in range(3 - a):
                at = (3 * n + a) * vecs
                gram = gram + total[at : at + vecs, b * vecs : (b + 1) * vecs]
        gram_ref[n] = gram


def vmem():
    return pl.BlockSpec(memory_space=pltpu.VMEM)


def smem():
    return pl.BlockSpec(memory_space=pltpu.SMEM)


def params():
    return pltpu.CompilerParams(vmem_limit_bytes=24 * 1024 * 1024)


def local(vectors, stiffness, attach, live, pair_harm, mistune):
    blades = pair_harm.shape[0] * 2
    slot_count, vecs, width = vectors.shape
    harm_size, grp_size = lax.axis_size("harm"), lax.axis_size("grp")
    me = lax.axis_index("harm")
    own_slots = me * slot_count + jnp.arange(slot_count, dtype=jnp.int32)
    theta, coup, _, _ = slot_tables(pair_harm, own_slots, blades)
    coef = jnp.concatenate([2.0 + 2.0 * (1.0 - jnp.cos(theta)), coup])

    ends = grp_size - 1
    low_edge = lax.ppermute(vectors[:, :, -1:], "grp", [(i, i + 1) for i in range(ends)])
    high_edge = lax.ppermute(vectors[:, :, :1], "grp", [(i + 1, i) for i in range(ends)])
    blank = jnp.zeros((slot_count, vecs, LANES - 2), jnp.float32)
    wide = jnp.concatenate([vectors, high_edge, blank, low_edge], axis=2)
    half = harm_size // 2
    partner = lax.ppermute(wide, "harm", [(i, i ^ half) for i in range(harm_size)])

    attach_tiles = attach.reshape(-1, LANES)
    packed = pl.pallas_call(
        gather_kernel,
        out_shape=jax.ShapeDtypeStruct((4 * harm_size, LANES), jnp.float32),
        in_specs=[vmem(), vmem()],
        out_specs=vmem(),
        compiler_params=params(),
        name="gather_rows",
    )(attach_tiles, vectors)
    recv = lax.all_to_all(packed.reshape(harm_size, 4, LANES), "harm", 0, 0)

    order = jnp.concatenate([jnp.arange(k, blades, slot_count, dtype=jnp.int32) for k in range(slot_count)])
    theta_all, _, harmonic_all, imag_all = slot_tables(pair_harm, order, blades)
    basis = basis_table(theta_all, harmonic_all, imag_all, blades)
    where = jnp.stack([me.astype(jnp.int32), live[0]])
    back = pl.pallas_call(
        blade_kernel,
        out_shape=jax.ShapeDtypeStruct((4 * harm_size, LANES), jnp.float32),
        in_specs=[smem(), vmem(), vmem(), vmem(), vmem()],
        out_specs=vmem(),
        compiler_params=params(),
        name="blades",
    )(where, recv.reshape(4 * harm_size, LANES), mistune.reshape(-1, LANES), basis, basis.T)
    back = lax.all_to_all(back.reshape(harm_size, 4, LANES), "harm", 0, 0)

    tiles = width // LANES
    image, gram = pl.pallas_call(
        final_kernel,
        out_shape=(
            jax.ShapeDtypeStruct(vectors.shape, jnp.float32),
            jax.ShapeDtypeStruct((2, vecs, vecs), jnp.float32),
        ),
        in_specs=[smem()] + [vmem()] * 5,
        out_specs=(vmem(), vmem()),
        scratch_shapes=[
            pltpu.VMEM((2, tiles, LANES), jnp.int32),
            pltpu.VMEM((4 * attach.shape[0] // LANES, OCT, LANES), jnp.float32),
        ],
        compiler_params=params(),
        name="image_gram",
    )(coef, attach.reshape(1, -1), stiffness.reshape(-1, LANES), wide, partner, back.reshape(4 * harm_size, LANES))

    part = gram.reshape(1, 4, LANES)
    part = lax.all_to_all(jnp.broadcast_to(part, (grp_size, 4, LANES)), "grp", 0, 0)
    part = jnp.sum(part, axis=0, keepdims=True)
    part = lax.all_to_all(jnp.broadcast_to(part, (harm_size, 4, LANES)), "harm", 0, 0)
    return (image, jnp.sum(part, axis=0).reshape(2, vecs, vecs))


def solution(mesh):
    in_specs = (P("harm", None, "grp"), P("grp"), P("grp"), P("grp"), P(), P(None, "grp", None))
    out_specs = (P("harm", None, "grp"), P())
    return jax.shard_map(local, mesh=mesh, in_specs=in_specs, out_specs=out_specs, check_vma=False)
```

```python
import math

import jax
import jax.numpy as jnp
from jax import lax
from jax.experimental import pallas as pl
from jax.experimental.pallas import tpu as pltpu
from jax.sharding import PartitionSpec as P

LANES = 128
OCT = 8
PIECE = 16


def iota(shape, dim):
    return lax.broadcasted_iota(jnp.int32, shape, dim)


def pick(tile, index):
    return jnp.take_along_axis(tile, index, axis=1, mode="promise_in_bounds")


def swap_blocks(tile):
    sub = iota(tile.shape, 0)
    block = iota(tile.shape, 1) // PIECE
    for bit in (1, 2, 4):
        from_low = pltpu.roll(pltpu.roll(tile, bit, 0), LANES - PIECE * bit, 1)
        from_high = pltpu.roll(pltpu.roll(tile, OCT - bit, 0), PIECE * bit, 1)
        s, b = (sub & bit) != 0, (block & bit) != 0
        tile = jnp.where(s & ~b, from_low, jnp.where(~s & b, from_high, tile))
    return tile


NT = (((1,), (1,)), ((), ()))
TN = (((0,), (0,)), ((), ()))


def dot_f32(a, b, dims):
    return lax.dot_general(a, b, dims, precision=lax.Precision.HIGHEST, preferred_element_type=jnp.float32)


def split(x, parts):
    out = []
    for _ in range(parts):
        out.append(x.astype(jnp.bfloat16))
        x = x - out[-1].astype(jnp.float32)
    return out


def angle_of(harmonic, imag, slots):
    wide = 2.0 * math.pi * harmonic.astype(jnp.float32) / slots
    return jnp.where(harmonic == 0, jnp.where(imag, math.pi, 0.0), wide)


def harm_index():
    return lax.axis_index("y") * lax.axis_size("z") + lax.axis_index("z")


def own_terms(pair_ref, k2):
    half = pair_ref.shape[0]
    slot = 2 * harm_index() + k2
    harmonic = jnp.full((OCT, LANES), pair_ref[lax.rem(slot, half)], jnp.int32)
    imag = jnp.full((OCT, LANES), slot, jnp.int32) >= half
    theta = angle_of(harmonic, imag, 2 * half)
    coup = jnp.where(harmonic == 0, 0.0, jnp.where(imag, -1.0, 1.0) * jnp.sin(theta))
    return 2.0 + 2.0 * (1.0 - jnp.cos(theta)), coup


OCTETS = [(j // 2, slice(OCT * (j % 2), OCT * (j % 2) + OCT)) for j in range(4)]


def fetch(attach_ref, t_ref, g_ref):
    group = 16

    def step(n, carry):
        for u in range(group):
            at = attach_ref[n * group + u]
            g_ref[pl.ds(pl.multiple_of(n * group, group) + u, 1), :] = t_ref[pl.ds(at, 1), :]
        return carry

    lax.fori_loop(0, attach_ref.shape[0] // group, step, 0)


def gather_kernel(attach_ref, v_ref, out_ref, t_ref, g_ref):
    def step(i, carry):
        here = pl.ds(pl.multiple_of(i * LANES, LANES), LANES)
        t_ref[here, :] = jnp.concatenate([v_ref[k2, o, here] for k2, o in OCTETS], axis=0).T
        return carry

    lax.fori_loop(0, v_ref.shape[2] // LANES, step, 0, unroll=8)
    fetch(attach_ref, t_ref, g_ref)
    owners = out_ref.shape[0] // 4
    part = iota((owners, LANES), 1) // 32
    for m in range(4):
        out = None
        for b in range(4):
            x = jnp.concatenate([g_ref[pl.ds(4 * b + m, owners, stride=PIECE), :]] * 4, axis=1)
            out = x if out is None else jnp.where(part == b, x, out)
        out_ref[pl.ds(m, owners, stride=4), :] = out


def table_kernel(pair_ref, attach_ref, partner_ref, basis_ref, inv_ref):
    tiles, rows = inv_ref.shape[1], attach_ref.shape[1]
    attach = attach_ref[...]
    r = iota((1, rows), 1)
    in_tile = (iota((tiles, rows), 0) == (attach >> 7)).astype(jnp.float32).astype(jnp.bfloat16)
    in_lane = iota((LANES, rows), 0) == (attach & (LANES - 1))
    for n, value in enumerate(((r >> 7) + 1, r & (LANES - 1))):
        weighted = jnp.where(in_lane, value.astype(jnp.float32), 0.0).astype(jnp.bfloat16)
        inv_ref[n] = lax.dot_general(in_tile, weighted, NT, preferred_element_type=jnp.float32).astype(jnp.int32)

    half = pair_ref.shape[1]
    slots = 2 * half
    pairs = jnp.broadcast_to(jnp.concatenate([pair_ref[...]] * 2, axis=1), (OCT, slots))
    lane = iota((OCT, slots), 1)
    slot = 2 * (lane & (half - 1)) + lane // half
    harmonic = pick(pairs, slot & (half - 1))
    imag = slot >= half
    theta = angle_of(harmonic, imag, slots)
    for n in range(slots // OCT):
        angle = (iota((OCT, slots), 0) + OCT * n).astype(jnp.float32) * theta
        cosine = jnp.cos(angle)
        wide = math.sqrt(2.0 / slots) * jnp.where(imag, jnp.sin(angle), cosine)
        basis_ref[OCT * n : OCT * (n + 1), :] = jnp.where(harmonic == 0, cosine / math.sqrt(slots), wide)


def shifted(ref, k2, o, i, count, low, high):
    here = pl.ds(pl.multiple_of(i * LANES, LANES), LANES)
    after = pl.ds(pl.multiple_of(jnp.minimum(i + 1, count - 1) * LANES, LANES), LANES)
    before = pl.ds(pl.multiple_of(jnp.maximum(i - 1, 0) * LANES, LANES), LANES)
    lane = iota((OCT, LANES), 1)
    v = ref[k2, o, here]
    prev = jnp.where(i == 0, low, ref[k2, o, before])
    follow = jnp.where(i == count - 1, high, ref[k2, o, after])
    lo = pltpu.roll(jnp.where(lane == LANES - 1, prev, v), 1, 1)
    hi = pltpu.roll(jnp.where(lane == 0, follow, v), LANES - 1, 1)
    return v, lo, hi


def adjust_kernel(pair_ref, attach_ref, stiff_ref, v_ref, p_ref, low_ref, high_ref, p_edge_ref, adj_ref, gram_ref, cols_ref, t_ref, g_ref):
    tiles, vecs, per = stiff_ref.shape[0], v_ref.shape[1], 4
    terms = [own_terms(pair_ref, k2) for k2 in range(2)]

    def edge(ref, k2, o, n):
        return jnp.broadcast_to(ref[k2, o, n : n + 1], (OCT, LANES))

    low = [edge(low_ref, k2, o, 0) for k2, o in OCTETS]
    high = [edge(high_ref, k2, o, 0) for k2, o in OCTETS]
    p_low = [edge(p_edge_ref, k2, o, 0) for k2, o in OCTETS]
    p_high = [edge(p_edge_ref, k2, o, 1) for k2, o in OCTETS]

    def step(g, gram):
        vs, ws = [], []
        for t in range(per):
            i = g * per + t
            here = pl.ds(pl.multiple_of(i * LANES, LANES), LANES)
            stiff = jnp.broadcast_to(stiff_ref[pl.ds(i, 1), :], (OCT, LANES))
            v_tile, w_tile = [], []
            for j, (k2, o) in enumerate(OCTETS):
                v, lo, hi = shifted(v_ref, k2, o, i, tiles, low[j], high[j])
                _, p_lo, p_hi = shifted(p_ref, k2, o, i, tiles, p_low[j], p_high[j])
                w = (terms[k2][0] + stiff) * v - lo - hi + terms[k2][1] * (p_hi - p_lo)
                adj_ref[k2, o, here] = w
                v_tile.append(v)
                w_tile.append(w)
            t_ref[here, :] = jnp.concatenate(v_tile + w_tile, axis=0).T
            vs.append(jnp.concatenate(v_tile, axis=0))
            ws.append(jnp.concatenate(w_tile, axis=0))
        v, w = jnp.concatenate(vs, axis=1), jnp.concatenate(ws, axis=1)
        for k2 in range(2):
            own = slice(vecs * k2, vecs * (k2 + 1))
            w3 = split(w[own], 3)
            left = jnp.concatenate(split(v[own], 3) + w3, axis=0)
            gram = gram + lax.dot_general(left, jnp.concatenate(w3, axis=0), NT, preferred_element_type=jnp.float32)
        return gram

    total = lax.fori_loop(0, tiles // per, step, jnp.zeros((6 * vecs, 3 * vecs), jnp.float32), unroll=2)
    for n in range(2):
        gram = jnp.zeros((vecs, vecs), jnp.float32)
        for a in range(3):
            for b in range(3 - a):
                at = (3 * n + a) * vecs
                gram = gram + total[at : at + vecs, b * vecs : (b + 1) * vecs]
        gram_ref[n * vecs : (n + 1) * vecs, :] = gram
    fetch(attach_ref, t_ref, g_ref)
    for c in range(cols_ref.shape[1] // LANES):
        here = slice(LANES * c, LANES * (c + 1))
        cols_ref[:, here] = g_ref[here, :].T


def blade_kernel(live_ref, recv_ref, mistune_ref, basis_ref, out_ref):
    me, live = harm_index(), live_ref[0]
    owners = out_ref.shape[0] // 4
    blades = 2 * owners
    slab = [recv_ref[pl.ds(m, owners, stride=4), :] for m in range(4)]
    piece = iota((owners, LANES), 1) // PIECE

    def arrived(k2):
        halves = []
        for half in range(2):
            out = None
            for n in range(OCT):
                r = OCT * half + n
                at = 2 * (r // 4) + k2
                tile = slab[r % 4] if at == n else pltpu.roll(slab[r % 4], (PIECE * (n - at)) % LANES, 1)
                out = tile if out is None else jnp.where(piece == n, tile, out)
            halves.append(out)
        return jnp.concatenate(halves, axis=1)

    wide = 2 * LANES
    alive = me * PIECE + iota((1, wide), 1) // PIECE < live
    rows = jnp.where(alive, jnp.concatenate([arrived(0), arrived(1)], axis=0), 0.0)
    mm = (((1,), (0,)), ((), ()))
    blade = dot_f32(basis_ref[...], rows, mm)
    chunk = mistune_ref[pl.ds(me // OCT, blades, stride=OCT), :]
    index = lax.rem(me, OCT) * PIECE + iota((blades, LANES), 1) // PIECE
    stiff = jnp.concatenate([pick(chunk, index), pick(chunk, index + OCT)], axis=1)
    back = jnp.where(alive, dot_f32(basis_ref[...], stiff * blade, TN), 0.0)
    down, across = iota((wide, wide), 0), iota((wide, wide), 1)
    swap = ((down & (PIECE - 1)) == across // PIECE) & (down // PIECE == (across & (PIECE - 1)))
    turned = dot_f32(back, swap.astype(jnp.float32), mm)
    for j in range(4):
        k2, vh = j // 2, j % 2
        out_ref[pl.ds(j, owners, stride=4), :] = turned[owners * k2 : owners * (k2 + 1), LANES * vh : LANES * (vh + 1)]


def cross_kernel(recv_ref, cols_ref, gram_ref, total_ref, back_ref):
    vecs, chunks = gram_ref.shape[1], cols_ref.shape[1] // LANES
    tiles = [[swap_blocks(recv_ref[pl.ds(4 * OCT * c + j, OCT, stride=4), :]) for c in range(chunks)] for j in range(4)]
    total = gram_ref[...]
    for k2 in range(2):
        both = []
        for j in (2 * k2, 2 * k2 + 1):
            for c in range(chunks):
                back_ref[4 * c + j] = tiles[j][c]
            both.append(jnp.concatenate(tiles[j], axis=1))
        back = jnp.concatenate(both, axis=0)
        left = jnp.concatenate(
            [cols_ref[vecs * k2 : vecs * (k2 + 1), :], cols_ref[vecs * (k2 + 2) : vecs * (k2 + 3), :] + 0.5 * back], axis=0
        )
        term = dot_f32(left, back, NT)
        twice = dot_f32(back, left[vecs:], NT)
        total = total + term + jnp.concatenate([jnp.zeros_like(twice), twice], axis=0)
    total_ref[...] = total


def image_kernel(inv_ref, adj_ref, back_ref, image_ref):
    tiles, chunks = inv_ref.shape[1], back_ref.shape[0] // 4

    def step(i, carry):
        here = pl.ds(pl.multiple_of(i * LANES, LANES), LANES)
        chunk = jnp.broadcast_to(inv_ref[0, pl.ds(i, 1), :], (OCT, LANES))
        index = jnp.broadcast_to(inv_ref[1, pl.ds(i, 1), :], (OCT, LANES))
        for j, (k2, o) in enumerate(OCTETS):
            back = jnp.zeros((OCT, LANES), jnp.float32)
            for c in range(chunks):
                back = jnp.where(chunk == c + 1, pick(back_ref[4 * c + j], index), back)
            image_ref[k2, o, here] = adj_ref[k2, o, here] + back
        return carry

    lax.fori_loop(0, tiles, step, 0, unroll=8)


def vmem():
    return pl.BlockSpec(memory_space=pltpu.VMEM)


def smem():
    return pl.BlockSpec(memory_space=pltpu.SMEM)


def params(mebibytes):
    return pltpu.CompilerParams(vmem_limit_bytes=mebibytes * 1024 * 1024)


def cost(microseconds):
    return pl.CostEstimate(flops=int(microseconds * 1e9), bytes_accessed=0, transcendentals=0)


HARM, GRP, PLANE = ("y", "z"), ("x", "core"), ("y", "x", "core")


def spread_sum(part, axes):
    count = math.prod(lax.axis_size(axis) for axis in axes)
    return jnp.sum(lax.all_to_all(jnp.broadcast_to(part[None], (count,) + part.shape), axes, 0, 0), axis=0)


def local(vectors, stiffness, attach, live, pair_harm, mistune):
    slot_count, vecs, width = vectors.shape
    rows, blades, tiles = attach.shape[0], 2 * pair_harm.shape[0], width // LANES
    harm_size = lax.axis_size("y") * lax.axis_size("z")
    grp_size = lax.axis_size("x") * lax.axis_size("core")
    block = jax.ShapeDtypeStruct(vectors.shape, jnp.float32)
    packed_rows = jax.ShapeDtypeStruct((4 * harm_size, LANES), jnp.float32)

    half = harm_size // 2
    to_partner = [(i, i ^ half) for i in range(harm_size)]
    partner = lax.ppermute(vectors, HARM, to_partner)
    ends = grp_size - 1
    low_edge = lax.ppermute(vectors[:, :, -1:], GRP, [(i, i + 1) for i in range(ends)])
    high_edge = lax.ppermute(vectors[:, :, :1], GRP, [(i + 1, i) for i in range(ends)])
    partner_edge = lax.ppermute(jnp.concatenate([low_edge, high_edge], axis=2), HARM, to_partner)

    packed = pl.pallas_call(
        gather_kernel,
        out_shape=packed_rows,
        in_specs=[smem(), vmem()],
        out_specs=vmem(),
        scratch_shapes=[pltpu.VMEM((width, 2 * vecs), jnp.float32), pltpu.VMEM((rows, 2 * vecs), jnp.float32)],
        compiler_params=params(16),
        cost_estimate=cost(5),
        name="gather",
    )(attach, vectors)
    recv = lax.all_to_all(packed.reshape(harm_size, 4, LANES), HARM, 0, 0)

    basis, inv = pl.pallas_call(
        table_kernel,
        out_shape=(
            jax.ShapeDtypeStruct((blades, blades), jnp.float32),
            jax.ShapeDtypeStruct((2, tiles, LANES), jnp.int32),
        ),
        in_specs=[vmem()] * 2 + [pl.BlockSpec(memory_space=pl.ANY)],
        out_specs=(vmem(),) * 2,
        compiler_params=params(8),
        cost_estimate=cost(60),
        name="tables",
    )(pair_harm.reshape(1, -1), attach.reshape(1, -1), partner)
    back = pl.pallas_call(
        blade_kernel,
        out_shape=packed_rows,
        in_specs=[smem()] + [vmem()] * 3,
        out_specs=vmem(),
        compiler_params=params(16),
        cost_estimate=cost(4),
        name="blades",
    )(live, recv.reshape(4 * harm_size, LANES), mistune.reshape(-1, LANES), basis)
    back = lax.all_to_all(back.reshape(harm_size, 4, LANES), HARM, 0, 0)

    adj, gram, cols = pl.pallas_call(
        adjust_kernel,
        out_shape=(
            block,
            jax.ShapeDtypeStruct((2 * vecs, vecs), jnp.float32),
            jax.ShapeDtypeStruct((4 * vecs, rows), jnp.float32),
        ),
        in_specs=[smem(), smem()] + [vmem()] * 6,
        out_specs=(vmem(),) * 3,
        scratch_shapes=[pltpu.VMEM((width, 4 * vecs), jnp.float32), pltpu.VMEM((rows, 4 * vecs), jnp.float32)],
        compiler_params=params(16),
        cost_estimate=cost(40),
        name="adjust",
    )(pair_harm, attach, stiffness.reshape(-1, LANES), vectors, partner, low_edge, high_edge, partner_edge)
    gram, back_tiles = pl.pallas_call(
        cross_kernel,
        out_shape=(
            jax.ShapeDtypeStruct((2 * vecs, vecs), jnp.float32),
            jax.ShapeDtypeStruct((4 * rows // LANES, OCT, LANES), jnp.float32),
        ),
        in_specs=[vmem()] * 3,
        out_specs=(vmem(),) * 2,
        compiler_params=params(8),
        cost_estimate=cost(1),
        name="cross",
    )(back.reshape(4 * harm_size, LANES), cols, gram)
    total = spread_sum(gram.reshape(4, LANES), PLANE)
    image = pl.pallas_call(
        image_kernel,
        out_shape=block,
        in_specs=[vmem()] * 3,
        out_specs=vmem(),
        compiler_params=params(8),
        cost_estimate=cost(20),
        name="image",
    )(inv, adj, back_tiles)
    total = spread_sum(total, ("z",))
    return (image, total.reshape(2, vecs, vecs))


def solution(mesh):
    shape = (4, 16, 4, 2)
    mesh = jax.sharding.Mesh(mesh.devices.reshape(shape), ("y", "z", "x", "core"))
    in_specs = (P(HARM, None, GRP), P(GRP), P(GRP), P(GRP), P(), P(None, GRP, None))
    out_specs = (P(HARM, None, GRP), P())
    return jax.shard_map(local, mesh=mesh, in_specs=in_specs, out_specs=out_specs, check_vma=False)
```

```python
import functools
import math

import jax
import jax.numpy as jnp
from jax import lax
from jax.experimental import pallas as pl
from jax.experimental.pallas import tpu as pltpu
from jax.sharding import PartitionSpec as P

LANES = 128
OCT = 8
PIECE = 16


def iota(shape, dim):
    return lax.broadcasted_iota(jnp.int32, shape, dim)


def pick(tile, index):
    return jnp.take_along_axis(tile, index, axis=1, mode="promise_in_bounds")


def swap_blocks(tile):
    sub = iota(tile.shape, 0)
    block = iota(tile.shape, 1) // PIECE
    for bit in (1, 2, 4):
        from_low = pltpu.roll(pltpu.roll(tile, bit, 0), LANES - PIECE * bit, 1)
        from_high = pltpu.roll(pltpu.roll(tile, OCT - bit, 0), PIECE * bit, 1)
        s, b = (sub & bit) != 0, (block & bit) != 0
        tile = jnp.where(s & ~b, from_low, jnp.where(~s & b, from_high, tile))
    return tile


NT = (((1,), (1,)), ((), ()))
TN = (((0,), (0,)), ((), ()))


def dot_f32(a, b, dims):
    return lax.dot_general(a, b, dims, precision=lax.Precision.HIGHEST, preferred_element_type=jnp.float32)


def split(x, parts):
    out = []
    for _ in range(parts):
        out.append(x.astype(jnp.bfloat16))
        x = x - out[-1].astype(jnp.float32)
    return out


def angle_of(harmonic, imag, slots):
    wide = 2.0 * math.pi * harmonic.astype(jnp.float32) / slots
    return jnp.where(harmonic == 0, jnp.where(imag, math.pi, 0.0), wide)


def harm_index():
    return lax.axis_index("y") * lax.axis_size("z") + lax.axis_index("z")


def own_terms(pair_ref, k2):
    half = pair_ref.shape[0]
    slot = 2 * harm_index() + k2
    harmonic = jnp.full((OCT, LANES), pair_ref[lax.rem(slot, half)], jnp.int32)
    imag = jnp.full((OCT, LANES), slot, jnp.int32) >= half
    theta = angle_of(harmonic, imag, 2 * half)
    coup = jnp.where(harmonic == 0, 0.0, jnp.where(imag, -1.0, 1.0) * jnp.sin(theta))
    return 2.0 + 2.0 * (1.0 - jnp.cos(theta)), coup


OCTETS = [(j // 2, slice(OCT * (j % 2), OCT * (j % 2) + OCT)) for j in range(4)]


def fetch(attach_ref, t_ref, g_ref):
    group = 64

    def step(n, carry):
        for u in range(group):
            at = attach_ref[n * group + u]
            g_ref[pl.ds(pl.multiple_of(n * group, group) + u, 1), :] = t_ref[pl.ds(at, 1), :]
        return carry

    lax.fori_loop(0, attach_ref.shape[0] // group, step, 0)


def gather_kernel(attach_ref, v_ref, out_ref, head_ref, tail_ref, t_ref, g_ref):
    head_ref[...] = v_ref[:, :, :1]
    tail_ref[...] = v_ref[:, :, v_ref.shape[2] - 1 :]

    def step(i, carry):
        here = pl.ds(pl.multiple_of(i * LANES, LANES), LANES)
        t_ref[here, :] = jnp.concatenate([v_ref[k2, o, here] for k2, o in OCTETS], axis=0).T
        return carry

    lax.fori_loop(0, v_ref.shape[2] // LANES, step, 0, unroll=32)
    fetch(attach_ref, t_ref, g_ref)
    owners = out_ref.shape[0] // 4
    part = iota((owners, LANES), 1) // 32
    for m in range(4):
        out = None
        for b in range(4):
            x = jnp.concatenate([g_ref[pl.ds(4 * b + m, owners, stride=PIECE), :]] * 4, axis=1)
            out = x if out is None else jnp.where(part == b, x, out)
        out_ref[pl.ds(m, owners, stride=4), :] = out


def table_kernel(pair_ref, attach_ref, partner_ref, basis_ref, inv_ref):
    tiles, rows = inv_ref.shape[1], attach_ref.shape[1]
    attach = attach_ref[...]
    r = iota((1, rows), 1)
    in_tile = (iota((tiles, rows), 0) == (attach >> 7)).astype(jnp.float32).astype(jnp.bfloat16)
    in_lane = iota((LANES, rows), 0) == (attach & (LANES - 1))
    for n, value in enumerate(((r >> 7) + 1, r & (LANES - 1))):
        weighted = jnp.where(in_lane, value.astype(jnp.float32), 0.0).astype(jnp.bfloat16)
        inv_ref[n] = lax.dot_general(in_tile, weighted, NT, preferred_element_type=jnp.float32).astype(jnp.int32)

    half = pair_ref.shape[1]
    slots = 2 * half
    pairs = jnp.broadcast_to(jnp.concatenate([pair_ref[...]] * 2, axis=1), (OCT, slots))
    lane = iota((OCT, slots), 1)
    slot = 2 * (lane & (half - 1)) + lane // half
    harmonic = pick(pairs, slot & (half - 1))
    imag = slot >= half
    theta = angle_of(harmonic, imag, slots)
    for n in range(slots // OCT):
        angle = (iota((OCT, slots), 0) + OCT * n).astype(jnp.float32) * theta
        cosine = jnp.cos(angle)
        wide = math.sqrt(2.0 / slots) * jnp.where(imag, jnp.sin(angle), cosine)
        basis_ref[OCT * n : OCT * (n + 1), :] = jnp.where(harmonic == 0, cosine / math.sqrt(slots), wide)


def shifted(ref, k2, o, i, count, low, high):
    here = pl.ds(pl.multiple_of(i * LANES, LANES), LANES)
    after = pl.ds(pl.multiple_of(jnp.minimum(i + 1, count - 1) * LANES, LANES), LANES)
    before = pl.ds(pl.multiple_of(jnp.maximum(i - 1, 0) * LANES, LANES), LANES)
    lane = iota((OCT, LANES), 1)
    v = ref[k2, o, here]
    prev = jnp.where(i == 0, low, ref[k2, o, before])
    follow = jnp.where(i == count - 1, high, ref[k2, o, after])
    lo = pltpu.roll(jnp.where(lane == LANES - 1, prev, v), 1, 1)
    hi = pltpu.roll(jnp.where(lane == 0, follow, v), LANES - 1, 1)
    return v, lo, hi


def adjusted(pair_ref, stiff_ref, v_ref, p_ref, edge_refs):
    tiles = stiff_ref.shape[0]
    terms = [own_terms(pair_ref, k2) for k2 in range(2)]
    if edge_refs is None:
        low = high = p_low = p_high = [jnp.zeros((OCT, LANES), jnp.float32)] * 4
    else:
        low, high = [[jnp.broadcast_to(ref[k2, o, :], (OCT, LANES)) for k2, o in OCTETS] for ref in edge_refs[:2]]
        p_low, p_high = [[jnp.broadcast_to(edge_refs[2][k2, o, n : n + 1], (OCT, LANES)) for k2, o in OCTETS] for n in range(2)]

    def at(i):
        stiff = jnp.broadcast_to(stiff_ref[pl.ds(i, 1), :], (OCT, LANES))
        v_tile, w_tile = [], []
        for j, (k2, o) in enumerate(OCTETS):
            v, lo, hi = shifted(v_ref, k2, o, i, tiles, low[j], high[j])
            _, p_lo, p_hi = shifted(p_ref, k2, o, i, tiles, p_low[j], p_high[j])
            v_tile.append(v)
            w_tile.append((terms[k2][0] + stiff) * v - lo - hi + terms[k2][1] * (p_hi - p_lo))
        return v_tile, w_tile

    return at


def adjust_kernel(pair_ref, attach_ref, stiff_ref, v_ref, p_ref, gram_ref, cols_ref, t_ref, g_ref):
    tiles, vecs, per = stiff_ref.shape[0], v_ref.shape[1], 8
    at = adjusted(pair_ref, stiff_ref, v_ref, p_ref, None)

    def step(g, gram):
        vs, ws = [], []
        for t in range(per):
            i = g * per + t
            v_tile, w_tile = at(i)
            here = pl.ds(pl.multiple_of(i * LANES, LANES), LANES)
            t_ref[here, :] = jnp.concatenate(v_tile + w_tile, axis=0).T
            vs.append(jnp.concatenate(v_tile, axis=0))
            ws.append(jnp.concatenate(w_tile, axis=0))
        v, w = jnp.concatenate(vs, axis=1), jnp.concatenate(ws, axis=1)
        for k2 in range(2):
            own = slice(vecs * k2, vecs * (k2 + 1))
            w3 = split(w[own], 3)
            left = jnp.concatenate(split(v[own], 3) + w3, axis=0)
            gram = gram + lax.dot_general(left, jnp.concatenate(w3, axis=0), NT, preferred_element_type=jnp.float32)
        return gram

    total = lax.fori_loop(0, tiles // per, step, jnp.zeros((6 * vecs, 3 * vecs), jnp.float32))
    for n in range(2):
        gram = jnp.zeros((vecs, vecs), jnp.float32)
        for a in range(3):
            for b in range(3 - a):
                at = (3 * n + a) * vecs
                gram = gram + total[at : at + vecs, b * vecs : (b + 1) * vecs]
        gram_ref[n * vecs : (n + 1) * vecs, :] = gram
    fetch(attach_ref, t_ref, g_ref)
    rows, last = g_ref.shape[0], t_ref.shape[0] - 1
    for c in range(rows // LANES):
        here = slice(LANES * c, LANES * (c + 1))
        cols_ref[:, here] = g_ref[here, :].T
    g_ref[:LANES, :] = jnp.zeros((LANES, g_ref.shape[1]), jnp.float32)
    g_ref[0:1, :] = t_ref[0:1, :]
    g_ref[1:2, :] = t_ref[last : last + 1, :]
    cols_ref[:, rows:] = g_ref[:LANES, :].T


def blade_kernel(live_ref, recv_ref, mistune_ref, basis_ref, low_ref, high_ref, out_ref, edge_ref):
    edge_ref[:, :, 0:1] = low_ref[...]
    edge_ref[:, :, 1:2] = high_ref[...]
    me, live = harm_index(), live_ref[0]
    owners = out_ref.shape[0] // 4
    blades = 2 * owners
    slab = [recv_ref[pl.ds(m, owners, stride=4), :] for m in range(4)]
    piece = iota((owners, LANES), 1) // PIECE

    def arrived(k2):
        halves = []
        for half in range(2):
            out = None
            for n in range(OCT):
                r = OCT * half + n
                at = 2 * (r // 4) + k2
                tile = slab[r % 4] if at == n else pltpu.roll(slab[r % 4], (PIECE * (n - at)) % LANES, 1)
                out = tile if out is None else jnp.where(piece == n, tile, out)
            halves.append(out)
        return jnp.concatenate(halves, axis=1)

    wide = 2 * LANES
    alive = me * PIECE + iota((1, wide), 1) // PIECE < live
    rows = jnp.where(alive, jnp.concatenate([arrived(0), arrived(1)], axis=0), 0.0)
    mm = (((1,), (0,)), ((), ()))
    blade = dot_f32(basis_ref[...], rows, mm)
    chunk = mistune_ref[pl.ds(me // OCT, blades, stride=OCT), :]
    index = lax.rem(me, OCT) * PIECE + iota((blades, LANES), 1) // PIECE
    stiff = jnp.concatenate([pick(chunk, index), pick(chunk, index + OCT)], axis=1)
    back = jnp.where(alive, dot_f32(basis_ref[...], stiff * blade, TN), 0.0)
    down, across = iota((wide, wide), 0), iota((wide, wide), 1)
    swap = ((down & (PIECE - 1)) == across // PIECE) & (down // PIECE == (across & (PIECE - 1)))
    turned = dot_f32(back, swap.astype(jnp.float32), mm)
    for j in range(4):
        k2, vh = j // 2, j % 2
        out_ref[pl.ds(j, owners, stride=4), :] = turned[owners * k2 : owners * (k2 + 1), LANES * vh : LANES * (vh + 1)]


def cross_kernel(width, pair_ref, attach_ref, recv_ref, cols_ref, gram_ref, low_ref, high_ref, p_edge_ref, total_ref, back_ref):
    vecs, rows = gram_ref.shape[1], attach_ref.shape[1]
    chunks = rows // LANES
    tiles = [[swap_blocks(recv_ref[pl.ds(4 * OCT * c + j, OCT, stride=4), :]) for c in range(chunks)] for j in range(4)]
    total = gram_ref[...]
    attach = attach_ref[...]
    at_first, at_last = attach == 0, attach == width - 1
    lane = iota((vecs, LANES), 1)
    for k2 in range(2):
        coup = own_terms(pair_ref, k2)[1][0:1, 0:1]
        both = []
        for j in (2 * k2, 2 * k2 + 1):
            for c in range(chunks):
                back_ref[4 * c + j] = tiles[j][c]
            both.append(jnp.concatenate(tiles[j], axis=1))
        back = jnp.concatenate(both, axis=0)
        first = -low_ref[k2] - coup * p_edge_ref[k2, :, 0:1]
        last = -high_ref[k2] + coup * p_edge_ref[k2, :, 1:2]
        outer = jnp.where(lane == 0, first, jnp.where(lane == 1, last, 0.0))
        at_rows = jnp.where(at_first, first, jnp.where(at_last, last, 0.0))
        more = jnp.concatenate([back, outer], axis=1)
        adj = cols_ref[vecs * (k2 + 2) : vecs * (k2 + 3), :] + jnp.concatenate([at_rows, jnp.zeros_like(outer)], axis=1)
        left = jnp.concatenate([cols_ref[vecs * k2 : vecs * (k2 + 1), :], adj + 0.5 * more], axis=0)
        term = dot_f32(left, more, NT)
        twice = dot_f32(more, left[vecs:], NT)
        total = total + term + jnp.concatenate([jnp.zeros_like(twice), twice], axis=0)
    total_ref[...] = total


def image_kernel(pair_ref, inv_ref, stiff_ref, v_ref, p_ref, low_ref, high_ref, p_edge_ref, back_ref, image_ref):
    tiles, chunks = inv_ref.shape[1], back_ref.shape[0] // 4
    at = adjusted(pair_ref, stiff_ref, v_ref, p_ref, (low_ref, high_ref, p_edge_ref))

    def step(i, carry):
        here = pl.ds(pl.multiple_of(i * LANES, LANES), LANES)
        chunk = jnp.broadcast_to(inv_ref[0, pl.ds(i, 1), :], (OCT, LANES))
        index = jnp.broadcast_to(inv_ref[1, pl.ds(i, 1), :], (OCT, LANES))
        _, w_tile = at(i)
        for j, (k2, o) in enumerate(OCTETS):
            back = jnp.zeros((OCT, LANES), jnp.float32)
            for c in range(chunks):
                back = jnp.where(chunk == c + 1, pick(back_ref[4 * c + j], index), back)
            image_ref[k2, o, here] = w_tile[j] + back
        return carry

    lax.fori_loop(0, tiles, step, 0, unroll=8)


def vmem():
    return pl.BlockSpec(memory_space=pltpu.VMEM)


def smem():
    return pl.BlockSpec(memory_space=pltpu.SMEM)


def params(mebibytes):
    return pltpu.CompilerParams(vmem_limit_bytes=mebibytes * 1024 * 1024)


def cost(microseconds):
    return pl.CostEstimate(flops=int(microseconds * 1e9), bytes_accessed=0, transcendentals=0)


HARM, GRP, PLANE = ("y", "z"), ("x", "core"), ("y", "x", "core")


def spread_sum(part, axes):
    count = math.prod(lax.axis_size(axis) for axis in axes)
    return jnp.sum(lax.all_to_all(jnp.broadcast_to(part[None], (count,) + part.shape), axes, 0, 0), axis=0)


def local(vectors, stiffness, attach, live, pair_harm, mistune):
    slot_count, vecs, width = vectors.shape
    rows, blades, tiles = attach.shape[0], 2 * pair_harm.shape[0], width // LANES
    harm_size = lax.axis_size("y") * lax.axis_size("z")
    grp_size = lax.axis_size("x") * lax.axis_size("core")
    block = jax.ShapeDtypeStruct(vectors.shape, jnp.float32)
    packed_rows = jax.ShapeDtypeStruct((4 * harm_size, LANES), jnp.float32)

    half = harm_size // 2
    to_partner = [(i, i ^ half) for i in range(harm_size)]
    partner = lax.ppermute(vectors, HARM, to_partner)
    edge = jax.ShapeDtypeStruct((slot_count, vecs, 1), jnp.float32)
    packed, head, tail = pl.pallas_call(
        gather_kernel,
        out_shape=(packed_rows, edge, edge),
        in_specs=[smem(), vmem()],
        out_specs=(vmem(),) * 3,
        scratch_shapes=[pltpu.VMEM((width, 2 * vecs), jnp.float32), pltpu.VMEM((rows, 2 * vecs), jnp.float32)],
        compiler_params=params(16),
        cost_estimate=cost(5),
        name="gather",
    )(attach, vectors)
    recv = lax.all_to_all(packed.reshape(harm_size, 4, LANES), HARM, 0, 0)
    ends = grp_size - 1
    low_edge = lax.ppermute(tail, GRP, [(i, i + 1) for i in range(ends)])
    high_edge = lax.ppermute(head, GRP, [(i + 1, i) for i in range(ends)])

    basis, inv = pl.pallas_call(
        table_kernel,
        out_shape=(
            jax.ShapeDtypeStruct((blades, blades), jnp.float32),
            jax.ShapeDtypeStruct((2, tiles, LANES), jnp.int32),
        ),
        in_specs=[vmem()] * 2 + [pl.BlockSpec(memory_space=pl.ANY)],
        out_specs=(vmem(),) * 2,
        compiler_params=params(8),
        cost_estimate=cost(60),
        name="tables",
    )(pair_harm.reshape(1, -1), attach.reshape(1, -1), partner)
    back, own_edge = pl.pallas_call(
        blade_kernel,
        out_shape=(packed_rows, jax.ShapeDtypeStruct((slot_count, vecs, 2), jnp.float32)),
        in_specs=[smem()] + [vmem()] * 5,
        out_specs=(vmem(),) * 2,
        compiler_params=params(16),
        cost_estimate=cost(4),
        name="blades",
    )(live, recv.reshape(4 * harm_size, LANES), mistune.reshape(-1, LANES), basis, low_edge, high_edge)
    back = lax.all_to_all(back.reshape(harm_size, 4, LANES), HARM, 0, 0)
    partner_edge = lax.ppermute(own_edge, HARM, to_partner)

    stiff = stiffness.reshape(-1, LANES)
    gram, cols = pl.pallas_call(
        adjust_kernel,
        out_shape=(
            jax.ShapeDtypeStruct((2 * vecs, vecs), jnp.float32),
            jax.ShapeDtypeStruct((4 * vecs, rows + LANES), jnp.float32),
        ),
        in_specs=[smem(), smem()] + [vmem()] * 3,
        out_specs=(vmem(),) * 2,
        scratch_shapes=[pltpu.VMEM((width, 4 * vecs), jnp.float32), pltpu.VMEM((rows, 4 * vecs), jnp.float32)],
        compiler_params=params(16),
        cost_estimate=cost(40),
        name="adjust",
    )(pair_harm, attach, stiff, vectors, partner)
    gram, back_tiles = pl.pallas_call(
        functools.partial(cross_kernel, width),
        out_shape=(
            jax.ShapeDtypeStruct((2 * vecs, vecs), jnp.float32),
            jax.ShapeDtypeStruct((4 * rows // LANES, OCT, LANES), jnp.float32),
        ),
        in_specs=[smem()] + [vmem()] * 7,
        out_specs=(vmem(),) * 2,
        compiler_params=params(8),
        cost_estimate=cost(1),
        name="cross",
    )(pair_harm, attach.reshape(1, -1), back.reshape(4 * harm_size, LANES), cols, gram, low_edge, high_edge, partner_edge)
    total = spread_sum(gram.reshape(4, LANES), PLANE)
    image = pl.pallas_call(
        image_kernel,
        out_shape=block,
        in_specs=[smem()] + [vmem()] * 8,
        out_specs=vmem(),
        compiler_params=params(8),
        cost_estimate=cost(20),
        name="image",
    )(pair_harm, inv, stiff, vectors, partner, low_edge, high_edge, partner_edge, back_tiles)
    total = spread_sum(total, ("z",))
    return (image, total.reshape(2, vecs, vecs))


def solution(mesh):
    shape = (4, 16, 4, 2)
    mesh = jax.sharding.Mesh(mesh.devices.reshape(shape), ("y", "z", "x", "core"))
    in_specs = (P(HARM, None, GRP), P(GRP), P(GRP), P(GRP), P(), P(None, GRP, None))
    out_specs = (P(HARM, None, GRP), P())
    return jax.shard_map(local, mesh=mesh, in_specs=in_specs, out_specs=out_specs, check_vma=False)
```

```python
import functools
import math

import jax
import jax.numpy as jnp
from jax import lax
from jax.experimental import pallas as pl
from jax.experimental.pallas import tpu as pltpu
from jax.sharding import PartitionSpec as P

LANES = 128
OCT = 8
PIECE = 16


def iota(shape, dim):
    return lax.broadcasted_iota(jnp.int32, shape, dim)


def pick(tile, index):
    return jnp.take_along_axis(tile, index, axis=1, mode="promise_in_bounds")


def swap_blocks(tile):
    sub = iota(tile.shape, 0)
    block = iota(tile.shape, 1) // PIECE
    for bit in (1, 2, 4):
        from_low = pltpu.roll(pltpu.roll(tile, bit, 0), LANES - PIECE * bit, 1)
        from_high = pltpu.roll(pltpu.roll(tile, OCT - bit, 0), PIECE * bit, 1)
        s, b = (sub & bit) != 0, (block & bit) != 0
        tile = jnp.where(s & ~b, from_low, jnp.where(~s & b, from_high, tile))
    return tile


NT = (((1,), (1,)), ((), ()))
TN = (((0,), (0,)), ((), ()))


def dot_f32(a, b, dims):
    return lax.dot_general(a, b, dims, precision=lax.Precision.HIGHEST, preferred_element_type=jnp.float32)


def split(x, parts):
    out = []
    for _ in range(parts):
        out.append(x.astype(jnp.bfloat16))
        x = x - out[-1].astype(jnp.float32)
    return out


def angle_of(harmonic, imag, slots):
    wide = 2.0 * math.pi * harmonic.astype(jnp.float32) / slots
    return jnp.where(harmonic == 0, jnp.where(imag, math.pi, 0.0), wide)


def harm_index():
    return lax.axis_index("y") * lax.axis_size("z") + lax.axis_index("z")


def own_terms(pair_ref, k2):
    half = pair_ref.shape[-1]
    slot = 2 * harm_index() + k2
    if len(pair_ref.shape) == 1:
        harmonic = jnp.full((OCT, LANES), pair_ref[lax.rem(slot, half)], jnp.int32)
    else:
        pairs = jnp.broadcast_to(jnp.concatenate([pair_ref[...]] * 2, axis=1), (OCT, LANES))
        harmonic = pick(pairs, jnp.full((OCT, LANES), lax.rem(slot, half), jnp.int32))
    imag = jnp.full((OCT, LANES), slot, jnp.int32) >= half
    theta = angle_of(harmonic, imag, 2 * half)
    coup = jnp.where(harmonic == 0, 0.0, jnp.where(imag, -1.0, 1.0) * jnp.sin(theta))
    return 2.0 + 2.0 * (1.0 - jnp.cos(theta)), coup


OCTETS = [(j // 2, slice(OCT * (j % 2), OCT * (j % 2) + OCT)) for j in range(4)]


def fetch(attach_ref, t_ref, g_ref):
    group = 64

    def step(n, carry):
        for u in range(group):
            at = attach_ref[n * group + u]
            g_ref[pl.ds(pl.multiple_of(n * group, group) + u, 1), :] = t_ref[pl.ds(at, 1), :]
        return carry

    lax.fori_loop(0, attach_ref.shape[0] // group, step, 0)


def gather_kernel(attach_hbm, v_hbm, out_ref, head_ref, tail_ref, attach_ref, v_ref, t_ref, g_ref, sems):
    parts, width = sems.shape[0] - 1, v_ref.shape[2]
    span = width // parts
    copies = [
        pltpu.make_async_copy(v_hbm.at[:, :, pl.ds(n * span, span)], v_ref.at[:, :, pl.ds(n * span, span)], sems.at[n])
        for n in range(parts)
    ]
    table = pltpu.make_async_copy(attach_hbm, attach_ref, sems.at[parts])
    for copy in copies[:1] + [table] + copies[1:]:
        copy.start()
    for n, copy in enumerate(copies):
        copy.wait()
        for i in range(n * span // LANES, (n + 1) * span // LANES):
            here = slice(LANES * i, LANES * (i + 1))
            t_ref[here, :] = jnp.concatenate([v_ref[k2, o, here] for k2, o in OCTETS], axis=0).T
    head_ref[...] = v_ref[:, :, :1]
    tail_ref[...] = v_ref[:, :, width - 1 :]
    table.wait()
    fetch(attach_ref, t_ref, g_ref)
    owners = out_ref.shape[0] // 4
    part = iota((owners, LANES), 1) // 32
    for m in range(4):
        out = None
        for b in range(4):
            x = jnp.concatenate([g_ref[pl.ds(4 * b + m, owners, stride=PIECE), :]] * 4, axis=1)
            out = x if out is None else jnp.where(part == b, x, out)
        out_ref[pl.ds(m, owners, stride=4), :] = out


def table_kernel(pair_ref, basis_ref, coup_ref):
    for k2 in range(2):
        coup_ref[k2] = own_terms(pair_ref, k2)[1]
    half = pair_ref.shape[1]
    slots = 2 * half
    pairs = jnp.broadcast_to(jnp.concatenate([pair_ref[...]] * 2, axis=1), (OCT, slots))
    lane = iota((OCT, slots), 1)
    slot = 2 * (lane & (half - 1)) + lane // half
    harmonic = pick(pairs, slot & (half - 1))
    imag = slot >= half
    theta = angle_of(harmonic, imag, slots)
    for n in range(slots // OCT):
        angle = (iota((OCT, slots), 0) + OCT * n).astype(jnp.float32) * theta
        cosine = jnp.cos(angle)
        wide = math.sqrt(2.0 / slots) * jnp.where(imag, jnp.sin(angle), cosine)
        basis_ref[OCT * n : OCT * (n + 1), :] = jnp.where(harmonic == 0, cosine / math.sqrt(slots), wide)


def shifted(ref, k2, o, i, count, low, high):
    here = pl.ds(pl.multiple_of(i * LANES, LANES), LANES)
    after = pl.ds(pl.multiple_of(jnp.minimum(i + 1, count - 1) * LANES, LANES), LANES)
    before = pl.ds(pl.multiple_of(jnp.maximum(i - 1, 0) * LANES, LANES), LANES)
    lane = iota((OCT, LANES), 1)
    v = ref[k2, o, here]
    prev = jnp.where(i == 0, low, ref[k2, o, before])
    follow = jnp.where(i == count - 1, high, ref[k2, o, after])
    lo = pltpu.roll(jnp.where(lane == LANES - 1, prev, v), 1, 1)
    hi = pltpu.roll(jnp.where(lane == 0, follow, v), LANES - 1, 1)
    return v, lo, hi


def adjusted(pair_ref, stiff_ref, v_ref, p_ref, edge_refs):
    tiles = stiff_ref.shape[0]
    terms = [own_terms(pair_ref, k2) for k2 in range(2)]
    if edge_refs is None:
        low = high = p_low = p_high = [jnp.zeros((OCT, LANES), jnp.float32)] * 4
    else:
        low, high = [[jnp.broadcast_to(ref[k2, o, :], (OCT, LANES)) for k2, o in OCTETS] for ref in edge_refs[:2]]
        p_low, p_high = [[jnp.broadcast_to(edge_refs[2][k2, o, n : n + 1], (OCT, LANES)) for k2, o in OCTETS] for n in range(2)]

    def at(i):
        stiff = jnp.broadcast_to(stiff_ref[pl.ds(i, 1), :], (OCT, LANES))
        v_tile, w_tile = [], []
        for j, (k2, o) in enumerate(OCTETS):
            v, lo, hi = shifted(v_ref, k2, o, i, tiles, low[j], high[j])
            _, p_lo, p_hi = shifted(p_ref, k2, o, i, tiles, p_low[j], p_high[j])
            v_tile.append(v)
            w_tile.append((terms[k2][0] + stiff) * v - lo - hi + terms[k2][1] * (p_hi - p_lo))
        return v_tile, w_tile

    return at


def adjust_kernel(pair_ref, attach_ref, stiff_ref, v_ref, p_ref, gram_ref, cols_ref, t_ref, g_ref):
    tiles, vecs, per = stiff_ref.shape[0], v_ref.shape[1], 8
    at = adjusted(pair_ref, stiff_ref, v_ref, p_ref, None)

    def step(g, gram):
        vs, ws = [], []
        for t in range(per):
            i = g * per + t
            v_tile, w_tile = at(i)
            here = pl.ds(pl.multiple_of(i * LANES, LANES), LANES)
            t_ref[here, :] = jnp.concatenate(v_tile + w_tile, axis=0).T
            vs.append(jnp.concatenate(v_tile, axis=0))
            ws.append(jnp.concatenate(w_tile, axis=0))
        v, w = jnp.concatenate(vs, axis=1), jnp.concatenate(ws, axis=1)
        for k2 in range(2):
            own = slice(vecs * k2, vecs * (k2 + 1))
            w3 = split(w[own], 3)
            left = jnp.concatenate(split(v[own], 3) + w3, axis=0)
            gram = gram + lax.dot_general(left, jnp.concatenate(w3, axis=0), NT, preferred_element_type=jnp.float32)
        return gram

    total = lax.fori_loop(0, tiles // per, step, jnp.zeros((6 * vecs, 3 * vecs), jnp.float32))
    for n in range(2):
        gram = jnp.zeros((vecs, vecs), jnp.float32)
        for a in range(3):
            for b in range(3 - a):
                at = (3 * n + a) * vecs
                gram = gram + total[at : at + vecs, b * vecs : (b + 1) * vecs]
        gram_ref[n * vecs : (n + 1) * vecs, :] = gram
    fetch(attach_ref, t_ref, g_ref)
    rows, last = g_ref.shape[0], t_ref.shape[0] - 1
    for c in range(rows // LANES):
        here = slice(LANES * c, LANES * (c + 1))
        cols_ref[:, here] = g_ref[here, :].T
    g_ref[:LANES, :] = jnp.zeros((LANES, g_ref.shape[1]), jnp.float32)
    g_ref[0:1, :] = t_ref[0:1, :]
    g_ref[1:2, :] = t_ref[last : last + 1, :]
    cols_ref[:, rows:] = g_ref[:LANES, :].T


def blade_kernel(live_ref, recv_ref, mistune_ref, basis_ref, out_ref, zero_ref):
    zero_ref[...] = jnp.zeros(zero_ref.shape, jnp.float32)
    me, live = harm_index(), live_ref[...]
    owners = out_ref.shape[0] // 4
    blades = 2 * owners
    slab = [recv_ref[pl.ds(m, owners, stride=4), :] for m in range(4)]
    piece = iota((owners, LANES), 1) // PIECE

    def arrived(k2):
        halves = []
        for half in range(2):
            out = None
            for n in range(OCT):
                r = OCT * half + n
                at = 2 * (r // 4) + k2
                tile = slab[r % 4] if at == n else pltpu.roll(slab[r % 4], (PIECE * (n - at)) % LANES, 1)
                out = tile if out is None else jnp.where(piece == n, tile, out)
            halves.append(out)
        return jnp.concatenate(halves, axis=1)

    wide = 2 * LANES
    alive = me * PIECE + iota((1, wide), 1) // PIECE < live
    rows = jnp.where(alive, jnp.concatenate([arrived(0), arrived(1)], axis=0), 0.0)
    mm = (((1,), (0,)), ((), ()))
    blade = dot_f32(basis_ref[...], rows, mm)
    chunk = mistune_ref[pl.ds(me // OCT, blades, stride=OCT), :]
    index = lax.rem(me, OCT) * PIECE + iota((blades, LANES), 1) // PIECE
    stiff = jnp.concatenate([pick(chunk, index), pick(chunk, index + OCT)], axis=1)
    back = jnp.where(alive, dot_f32(basis_ref[...], stiff * blade, TN), 0.0)
    down, across = iota((wide, wide), 0), iota((wide, wide), 1)
    swap = ((down & (PIECE - 1)) == across // PIECE) & (down // PIECE == (across & (PIECE - 1)))
    turned = dot_f32(back, swap.astype(jnp.float32), mm)
    for j in range(4):
        k2, vh = j // 2, j % 2
        out_ref[pl.ds(j, owners, stride=4), :] = turned[owners * k2 : owners * (k2 + 1), LANES * vh : LANES * (vh + 1)]


def cross_kernel(width, coup_ref, attach_ref, recv_ref, cols_ref, gram_ref, low_ref, high_ref, p_edge_ref, total_ref, back_ref):
    vecs, rows = gram_ref.shape[1], attach_ref.shape[1]
    chunks = rows // LANES
    tiles = [[swap_blocks(recv_ref[pl.ds(4 * OCT * c + j, OCT, stride=4), :]) for c in range(chunks)] for j in range(4)]
    attach = attach_ref[...]
    at_first, at_last = attach == 0, attach == width - 1
    lane = iota((vecs, LANES), 1)
    for k2 in range(2):
        coup = coup_ref[k2, 0:1, 0:1]
        both = []
        for j in (2 * k2, 2 * k2 + 1):
            for c in range(chunks):
                back_ref[4 * c + j] = tiles[j][c]
            both.append(jnp.concatenate(tiles[j], axis=1))
        back = jnp.concatenate(both, axis=0)
        first = -low_ref[k2] - coup * p_edge_ref[k2, :, 0:1]
        last = -high_ref[k2] + coup * p_edge_ref[k2, :, 1:2]
        outer = jnp.where(lane == 0, first, jnp.where(lane == 1, last, 0.0))
        at_rows = jnp.where(at_first, first, jnp.where(at_last, last, 0.0))
        more = jnp.concatenate([back, outer], axis=1)
        adj = cols_ref[vecs * (k2 + 2) : vecs * (k2 + 3), :] + jnp.concatenate([at_rows, jnp.zeros_like(outer)], axis=1)
        left = jnp.concatenate([cols_ref[vecs * k2 : vecs * (k2 + 1), :], adj + 0.5 * more], axis=0)
        term = dot_f32(left, more, NT)
        terms = term if k2 == 0 else terms + term
    unit = (iota((vecs, vecs), 0) == iota((vecs, vecs), 1)).astype(jnp.float32)
    twice = dot_f32(unit, terms[vecs:], NT)
    total_ref[...] = gram_ref[...] + terms + jnp.concatenate([jnp.zeros_like(twice), twice], axis=0)


def inverse(attach_ref, inv_ref):
    tiles, rows = inv_ref.shape[1], attach_ref.shape[1]
    attach = attach_ref[...]
    r = iota((1, rows), 1)
    in_tile = (iota((tiles, rows), 0) == (attach >> 7)).astype(jnp.float32).astype(jnp.bfloat16)
    in_lane = iota((LANES, rows), 0) == (attach & (LANES - 1))
    for n, value in enumerate(((r >> 7) + 1, r & (LANES - 1))):
        weighted = jnp.where(in_lane, value.astype(jnp.float32), 0.0).astype(jnp.bfloat16)
        inv_ref[n] = lax.dot_general(in_tile, weighted, NT, preferred_element_type=jnp.float32).astype(jnp.int32)


def image_kernel(pair_ref, attach_ref, stiff_ref, v_ref, p_ref, low_ref, high_ref, p_edge_ref, back_ref, image_ref, inv_ref):
    inverse(attach_ref, inv_ref)
    tiles, chunks = inv_ref.shape[1], back_ref.shape[0] // 4
    at = adjusted(pair_ref, stiff_ref, v_ref, p_ref, (low_ref, high_ref, p_edge_ref))

    def step(i, carry):
        here = pl.ds(pl.multiple_of(i * LANES, LANES), LANES)
        chunk = jnp.broadcast_to(inv_ref[0, pl.ds(i, 1), :], (OCT, LANES))
        index = jnp.broadcast_to(inv_ref[1, pl.ds(i, 1), :], (OCT, LANES))
        _, w_tile = at(i)
        for j, (k2, o) in enumerate(OCTETS):
            back = jnp.zeros((OCT, LANES), jnp.float32)
            for c in range(chunks):
                back = jnp.where(chunk == c + 1, pick(back_ref[4 * c + j], index), back)
            image_ref[k2, o, here] = w_tile[j] + back
        return carry

    lax.fori_loop(0, tiles, step, 0, unroll=8)


def vmem():
    return pl.BlockSpec(memory_space=pltpu.VMEM)


def smem():
    return pl.BlockSpec(memory_space=pltpu.SMEM)


def params(mebibytes):
    return pltpu.CompilerParams(vmem_limit_bytes=mebibytes * 1024 * 1024)


def cost(microseconds):
    return pl.CostEstimate(flops=int(microseconds * 1e9), bytes_accessed=0, transcendentals=0)


HARM, GRP, PLANE = ("y", "z"), ("x", "core"), ("y", "x", "core")


def spread_sum(part, axes):
    count = math.prod(lax.axis_size(axis) for axis in axes)
    return jnp.sum(lax.all_to_all(jnp.broadcast_to(part[None], (count,) + part.shape), axes, 0, 0), axis=0)


def local(vectors, stiffness, attach, live, pair_harm, mistune):
    slot_count, vecs, width = vectors.shape
    rows, blades, tiles = attach.shape[0], 2 * pair_harm.shape[0], width // LANES
    harm_size = lax.axis_size("y") * lax.axis_size("z")
    grp_size = lax.axis_size("x") * lax.axis_size("core")
    block = jax.ShapeDtypeStruct(vectors.shape, jnp.float32)
    packed_rows = jax.ShapeDtypeStruct((4 * harm_size, LANES), jnp.float32)

    half = harm_size // 2
    to_partner = [(i, i ^ half) for i in range(harm_size)]
    partner = lax.ppermute(vectors, HARM, to_partner)
    edge = jax.ShapeDtypeStruct((slot_count, vecs, 1), jnp.float32)
    packed, head, tail = pl.pallas_call(
        gather_kernel,
        out_shape=(
            packed_rows,
            edge,
            edge,
        ),
        in_specs=[pl.BlockSpec(memory_space=pltpu.HBM)] * 2,
        out_specs=(vmem(),) * 3,
        scratch_shapes=[
            pltpu.SMEM(attach.shape, jnp.int32),
            pltpu.VMEM(vectors.shape, jnp.float32),
            pltpu.VMEM((width, 2 * vecs), jnp.float32),
            pltpu.VMEM((rows, 2 * vecs), jnp.float32),
            pltpu.SemaphoreType.DMA((9,)),
        ],
        compiler_params=params(62),
        cost_estimate=cost(5),
        name="gather",
    )(attach, vectors)
    recv = lax.all_to_all(packed.reshape(harm_size, 4, LANES), HARM, 0, 0)
    ends = grp_size - 1
    low_edge = lax.ppermute(tail, GRP, [(i, i + 1) for i in range(ends)])
    high_edge = lax.ppermute(head, GRP, [(i + 1, i) for i in range(ends)])

    basis, coup = pl.pallas_call(
        table_kernel,
        out_shape=(
            jax.ShapeDtypeStruct((blades, blades), jnp.float32),
            jax.ShapeDtypeStruct((2, OCT, LANES), jnp.float32),
        ),
        in_specs=[vmem()],
        out_specs=(vmem(),) * 2,
        compiler_params=params(8),
        cost_estimate=cost(1),
        name="tables",
    )(pair_harm.reshape(1, -1))
    back, zero = pl.pallas_call(
        blade_kernel,
        out_shape=(packed_rows, jax.ShapeDtypeStruct((slot_count, vecs, 2), jnp.float32)),
        in_specs=[vmem()] * 4,
        out_specs=(vmem(),) * 2,
        compiler_params=params(16),
        cost_estimate=cost(1),
        name="blades",
    )(live.reshape(1, 1), recv.reshape(4 * harm_size, LANES), mistune.reshape(-1, LANES), basis)
    back = lax.all_to_all(back.reshape(harm_size, 4, LANES), HARM, 0, 0)
    partner_edge = lax.ppermute(jnp.concatenate([low_edge, high_edge], axis=2) + zero, HARM, to_partner)

    stiff = stiffness.reshape(-1, LANES)
    gram, cols = pl.pallas_call(
        adjust_kernel,
        out_shape=(
            jax.ShapeDtypeStruct((2 * vecs, vecs), jnp.float32),
            jax.ShapeDtypeStruct((4 * vecs, rows + LANES), jnp.float32),
        ),
        in_specs=[smem(), smem()] + [vmem()] * 3,
        out_specs=(vmem(),) * 2,
        scratch_shapes=[pltpu.VMEM((width, 4 * vecs), jnp.float32), pltpu.VMEM((rows, 4 * vecs), jnp.float32)],
        compiler_params=params(16),
        cost_estimate=cost(40),
        name="adjust",
    )(pair_harm, attach, stiff, vectors, partner)
    gram, back_tiles = pl.pallas_call(
        functools.partial(cross_kernel, width),
        out_shape=(
            jax.ShapeDtypeStruct((2 * vecs, vecs), jnp.float32),
            jax.ShapeDtypeStruct((4 * rows // LANES, OCT, LANES), jnp.float32),
        ),
        in_specs=[vmem()] * 8,
        out_specs=(vmem(),) * 2,
        compiler_params=params(8),
        cost_estimate=cost(1),
        name="cross",
    )(coup, attach.reshape(1, -1), back.reshape(4 * harm_size, LANES), cols, gram, low_edge, high_edge, partner_edge)
    total = spread_sum(gram.reshape(4, LANES), PLANE)
    image = pl.pallas_call(
        image_kernel,
        out_shape=block,
        in_specs=[smem()] + [vmem()] * 8,
        out_specs=vmem(),
        scratch_shapes=[pltpu.VMEM((2, tiles, LANES), jnp.int32)],
        compiler_params=params(8),
        cost_estimate=cost(20),
        name="image",
    )(pair_harm, attach.reshape(1, -1), stiff, vectors, partner, low_edge, high_edge, partner_edge, back_tiles)
    total = spread_sum(total, ("z",))
    return (image, total.reshape(2, vecs, vecs))


def solution(mesh):
    shape = (4, 16, 4, 2)
    mesh = jax.sharding.Mesh(mesh.devices.reshape(shape), ("y", "z", "x", "core"))
    in_specs = (P(HARM, None, GRP), P(GRP), P(GRP), P(GRP), P(), P(None, GRP, None))
    out_specs = (P(HARM, None, GRP), P())
    return jax.shard_map(local, mesh=mesh, in_specs=in_specs, out_specs=out_specs, check_vma=False)
```

```python
import functools
import math

import jax
import jax.numpy as jnp
from jax import lax
from jax.experimental import pallas as pl
from jax.experimental.pallas import tpu as pltpu
from jax.sharding import PartitionSpec as P

LANES = 128
OCT = 8
PIECE = 16


def iota(shape, dim):
    return lax.broadcasted_iota(jnp.int32, shape, dim)


def pick(tile, index):
    return jnp.take_along_axis(tile, index, axis=1, mode="promise_in_bounds")


def swap_blocks(tile):
    sub = iota(tile.shape, 0)
    block = iota(tile.shape, 1) // PIECE
    for bit in (1, 2, 4):
        from_low = pltpu.roll(pltpu.roll(tile, bit, 0), LANES - PIECE * bit, 1)
        from_high = pltpu.roll(pltpu.roll(tile, OCT - bit, 0), PIECE * bit, 1)
        s, b = (sub & bit) != 0, (block & bit) != 0
        tile = jnp.where(s & ~b, from_low, jnp.where(~s & b, from_high, tile))
    return tile


NT = (((1,), (1,)), ((), ()))
TN = (((0,), (0,)), ((), ()))


def dot_f32(a, b, dims):
    return lax.dot_general(a, b, dims, precision=lax.Precision.HIGHEST, preferred_element_type=jnp.float32)


def split(x, parts):
    out = []
    for _ in range(parts):
        out.append(x.astype(jnp.bfloat16))
        x = x - out[-1].astype(jnp.float32)
    return out


def angle_of(harmonic, imag, slots):
    wide = 2.0 * math.pi * harmonic.astype(jnp.float32) / slots
    return jnp.where(harmonic == 0, jnp.where(imag, math.pi, 0.0), wide)


def harm_index():
    return lax.axis_index("y") * lax.axis_size("z") + lax.axis_index("z")


def own_terms(pair_ref, k2):
    half = pair_ref.shape[-1]
    slot = 2 * harm_index() + k2
    if len(pair_ref.shape) == 1:
        harmonic = jnp.full((OCT, LANES), pair_ref[lax.rem(slot, half)], jnp.int32)
    else:
        pairs = jnp.broadcast_to(jnp.concatenate([pair_ref[...]] * 2, axis=1), (OCT, LANES))
        harmonic = pick(pairs, jnp.full((OCT, LANES), lax.rem(slot, half), jnp.int32))
    imag = jnp.full((OCT, LANES), slot, jnp.int32) >= half
    theta = angle_of(harmonic, imag, 2 * half)
    coup = jnp.where(harmonic == 0, 0.0, jnp.where(imag, -1.0, 1.0) * jnp.sin(theta))
    return 2.0 + 2.0 * (1.0 - jnp.cos(theta)), coup


OCTETS = [(j // 2, slice(OCT * (j % 2), OCT * (j % 2) + OCT)) for j in range(4)]


def fetch(attach_ref, t_ref, g_ref):
    group = 64

    def step(n, carry):
        for u in range(group):
            at = attach_ref[n * group + u]
            g_ref[pl.ds(pl.multiple_of(n * group, group) + u, 1), :] = t_ref[pl.ds(at, 1), :]
        return carry

    lax.fori_loop(0, attach_ref.shape[0] // group, step, 0)


def gather_kernel(attach_hbm, v_hbm, out_ref, head_ref, tail_ref, attach_ref, v_ref, t_ref, g_ref, sems):
    parts, width = sems.shape[0] - 1, v_ref.shape[2]
    span = width // parts
    copies = [
        pltpu.make_async_copy(v_hbm.at[:, :, pl.ds(n * span, span)], v_ref.at[:, :, pl.ds(n * span, span)], sems.at[n])
        for n in range(parts)
    ]
    table = pltpu.make_async_copy(attach_hbm, attach_ref, sems.at[parts])
    for copy in copies[:1] + [table] + copies[1:]:
        copy.start()
    for n, copy in enumerate(copies):
        copy.wait()
        for i in range(n * span // LANES, (n + 1) * span // LANES):
            here = slice(LANES * i, LANES * (i + 1))
            t_ref[here, :] = jnp.concatenate([v_ref[k2, o, here] for k2, o in OCTETS], axis=0).T
    head_ref[...] = v_ref[:, :, :1]
    tail_ref[...] = v_ref[:, :, width - 1 :]
    table.wait()
    fetch(attach_ref, t_ref, g_ref)
    owners = out_ref.shape[0] // 4
    part = iota((owners, LANES), 1) // 32
    for m in range(4):
        out = None
        for b in range(4):
            x = jnp.concatenate([g_ref[pl.ds(4 * b + m, owners, stride=PIECE), :]] * 4, axis=1)
            out = x if out is None else jnp.where(part == b, x, out)
        out_ref[pl.ds(m, owners, stride=4), :] = out


def table_kernel(pair_ref, basis_ref, coup_ref):
    for k2 in range(2):
        coup_ref[k2] = own_terms(pair_ref, k2)[1]
    half = pair_ref.shape[1]
    slots = 2 * half
    pairs = jnp.broadcast_to(jnp.concatenate([pair_ref[...]] * 2, axis=1), (OCT, slots))
    lane = iota((OCT, slots), 1)
    slot = 2 * (lane & (half - 1)) + lane // half
    harmonic = pick(pairs, slot & (half - 1))
    imag = slot >= half
    theta = angle_of(harmonic, imag, slots)
    for n in range(slots // OCT):
        angle = (iota((OCT, slots), 0) + OCT * n).astype(jnp.float32) * theta
        cosine = jnp.cos(angle)
        wide = math.sqrt(2.0 / slots) * jnp.where(imag, jnp.sin(angle), cosine)
        basis_ref[OCT * n : OCT * (n + 1), :] = jnp.where(harmonic == 0, cosine / math.sqrt(slots), wide)


def shifted(ref, k2, o, i, count, low, high):
    here = pl.ds(pl.multiple_of(i * LANES, LANES), LANES)
    after = pl.ds(pl.multiple_of(jnp.minimum(i + 1, count - 1) * LANES, LANES), LANES)
    before = pl.ds(pl.multiple_of(jnp.maximum(i - 1, 0) * LANES, LANES), LANES)
    lane = iota((OCT, LANES), 1)
    v = ref[k2, o, here]
    prev = jnp.where(i == 0, low, ref[k2, o, before])
    follow = jnp.where(i == count - 1, high, ref[k2, o, after])
    lo = pltpu.roll(jnp.where(lane == LANES - 1, prev, v), 1, 1)
    hi = pltpu.roll(jnp.where(lane == 0, follow, v), LANES - 1, 1)
    return v, lo, hi


def adjusted(pair_ref, stiff_ref, v_ref, p_ref, edge_refs):
    tiles = stiff_ref.shape[0]
    terms = [own_terms(pair_ref, k2) for k2 in range(2)]
    if edge_refs is None:
        low = high = p_low = p_high = [jnp.zeros((OCT, LANES), jnp.float32)] * 4
    else:
        low, high = [[jnp.broadcast_to(ref[k2, o, :], (OCT, LANES)) for k2, o in OCTETS] for ref in edge_refs[:2]]
        p_low, p_high = [[jnp.broadcast_to(edge_refs[2][k2, o, n : n + 1], (OCT, LANES)) for k2, o in OCTETS] for n in range(2)]

    def at(i):
        stiff = jnp.broadcast_to(stiff_ref[pl.ds(i, 1), :], (OCT, LANES))
        v_tile, w_tile = [], []
        for j, (k2, o) in enumerate(OCTETS):
            v, lo, hi = shifted(v_ref, k2, o, i, tiles, low[j], high[j])
            _, p_lo, p_hi = shifted(p_ref, k2, o, i, tiles, p_low[j], p_high[j])
            v_tile.append(v)
            w_tile.append((terms[k2][0] + stiff) * v - lo - hi + terms[k2][1] * (p_hi - p_lo))
        return v_tile, w_tile

    return at


def adjust_kernel(pair_ref, attach_ref, stiff_ref, v_ref, p_ref, gram_ref, cols_ref, t_ref, g_ref):
    tiles, vecs, per = stiff_ref.shape[0], v_ref.shape[1], 8
    at = adjusted(pair_ref, stiff_ref, v_ref, p_ref, None)

    def step(g, gram):
        vs, ws = [], []
        for t in range(per):
            i = g * per + t
            v_tile, w_tile = at(i)
            here = pl.ds(pl.multiple_of(i * LANES, LANES), LANES)
            t_ref[here, :] = jnp.concatenate(v_tile + w_tile, axis=0).T
            vs.append(jnp.concatenate(v_tile, axis=0))
            ws.append(jnp.concatenate(w_tile, axis=0))
        v, w = jnp.concatenate(vs, axis=1), jnp.concatenate(ws, axis=1)
        for k2 in range(2):
            own = slice(vecs * k2, vecs * (k2 + 1))
            w3 = split(w[own], 3)
            left = jnp.concatenate(split(v[own], 3) + w3, axis=0)
            gram = gram + lax.dot_general(left, jnp.concatenate(w3, axis=0), NT, preferred_element_type=jnp.float32)
        return gram

    total = lax.fori_loop(0, tiles // per, step, jnp.zeros((6 * vecs, 3 * vecs), jnp.float32))
    for n in range(2):
        gram = jnp.zeros((vecs, vecs), jnp.float32)
        for a in range(3):
            for b in range(3 - a):
                at = (3 * n + a) * vecs
                gram = gram + total[at : at + vecs, b * vecs : (b + 1) * vecs]
        gram_ref[n * vecs : (n + 1) * vecs, :] = gram
    fetch(attach_ref, t_ref, g_ref)
    rows, last = g_ref.shape[0], t_ref.shape[0] - 1
    for c in range(rows // LANES):
        here = slice(LANES * c, LANES * (c + 1))
        cols_ref[:, here] = g_ref[here, :].T
    g_ref[:LANES, :] = jnp.zeros((LANES, g_ref.shape[1]), jnp.float32)
    g_ref[0:1, :] = t_ref[0:1, :]
    g_ref[1:2, :] = t_ref[last : last + 1, :]
    cols_ref[:, rows:] = g_ref[:LANES, :].T


def blade_kernel(live_ref, recv_ref, mistune_ref, basis_ref, low_ref, high_ref, out_ref):
    me, live = harm_index(), live_ref[...]
    owners = out_ref.shape[0] // 5
    blades = 2 * owners
    slab = [recv_ref[pl.ds(m, owners, stride=4), :] for m in range(4)]
    piece = iota((owners, LANES), 1) // PIECE

    def arrived(k2):
        halves = []
        for half in range(2):
            out = None
            for n in range(OCT):
                r = OCT * half + n
                at = 2 * (r // 4) + k2
                tile = slab[r % 4] if at == n else pltpu.roll(slab[r % 4], (PIECE * (n - at)) % LANES, 1)
                out = tile if out is None else jnp.where(piece == n, tile, out)
            halves.append(out)
        return jnp.concatenate(halves, axis=1)

    wide = 2 * LANES
    alive = me * PIECE + iota((1, wide), 1) // PIECE < live
    rows = jnp.where(alive, jnp.concatenate([arrived(0), arrived(1)], axis=0), 0.0)
    mm = (((1,), (0,)), ((), ()))
    blade = dot_f32(basis_ref[...], rows, mm)
    chunk = mistune_ref[pl.ds(me // OCT, blades, stride=OCT), :]
    index = lax.rem(me, OCT) * PIECE + iota((blades, LANES), 1) // PIECE
    stiff = jnp.concatenate([pick(chunk, index), pick(chunk, index + OCT)], axis=1)
    back = jnp.where(alive, dot_f32(basis_ref[...], stiff * blade, TN), 0.0)
    down, across = iota((wide, wide), 0), iota((wide, wide), 1)
    swap = ((down & (PIECE - 1)) == across // PIECE) & (down // PIECE == (across & (PIECE - 1)))
    turned = dot_f32(back, swap.astype(jnp.float32), mm)
    for j in range(4):
        k2, vh = j // 2, j % 2
        out_ref[pl.ds(j, owners, stride=5), :] = turned[owners * k2 : owners * (k2 + 1), LANES * vh : LANES * (vh + 1)]
    column = jnp.concatenate([ref[k2] for ref in (low_ref, high_ref) for k2 in range(2)], axis=0)
    shape = (column.shape[0], LANES)
    row = jnp.sum(jnp.where(iota(shape, 0) == iota(shape, 1), column, 0.0), axis=0, keepdims=True)
    out_ref[pl.ds(4, owners, stride=5), :] = jnp.broadcast_to(row, (owners, LANES))


def cross_kernel(width, coup_ref, attach_ref, recv_ref, cols_ref, gram_ref, low_ref, high_ref, total_ref, back_ref, p_edge_ref):
    vecs, rows = gram_ref.shape[1], attach_ref.shape[1]
    chunks = rows // LANES
    tiles = [[swap_blocks(recv_ref[pl.ds(5 * OCT * c + j, OCT, stride=5), :]) for c in range(chunks)] for j in range(4)]
    owners, me = recv_ref.shape[0] // 5, harm_index()
    half = owners // 2
    partner = jnp.where(me < half, me + half, me - half)
    shape = (4 * vecs, LANES)
    row = jnp.broadcast_to(recv_ref[pl.ds(5 * partner + 4, 1), :], shape)
    outside = jnp.sum(jnp.where(iota(shape, 0) == iota(shape, 1), row, 0.0), axis=1, keepdims=True)
    for n in range(2):
        for k2 in range(2):
            p_edge_ref[k2, :, n : n + 1] = outside[vecs * (2 * n + k2) : vecs * (2 * n + k2 + 1)]
    attach = attach_ref[...]
    at_first, at_last = attach == 0, attach == width - 1
    lane = iota((vecs, LANES), 1)
    for k2 in range(2):
        coup = coup_ref[k2, 0:1, 0:1]
        both = []
        for j in (2 * k2, 2 * k2 + 1):
            for c in range(chunks):
                back_ref[4 * c + j] = tiles[j][c]
            both.append(jnp.concatenate(tiles[j], axis=1))
        back = jnp.concatenate(both, axis=0)
        first = -low_ref[k2] - coup * outside[vecs * k2 : vecs * (k2 + 1)]
        last = -high_ref[k2] + coup * outside[vecs * (k2 + 2) : vecs * (k2 + 3)]
        outer = jnp.where(lane == 0, first, jnp.where(lane == 1, last, 0.0))
        at_rows = jnp.where(at_first, first, jnp.where(at_last, last, 0.0))
        more = jnp.concatenate([back, outer], axis=1)
        adj = cols_ref[vecs * (k2 + 2) : vecs * (k2 + 3), :] + jnp.concatenate([at_rows, jnp.zeros_like(outer)], axis=1)
        left = jnp.concatenate([cols_ref[vecs * k2 : vecs * (k2 + 1), :], adj + 0.5 * more], axis=0)
        term = dot_f32(left, more, NT)
        terms = term if k2 == 0 else terms + term
    unit = (iota((vecs, vecs), 0) == iota((vecs, vecs), 1)).astype(jnp.float32)
    twice = dot_f32(unit, terms[vecs:], NT)
    total_ref[...] = gram_ref[...] + terms + jnp.concatenate([jnp.zeros_like(twice), twice], axis=0)


def inverse(attach_ref, inv_ref):
    tiles, rows = inv_ref.shape[1], attach_ref.shape[1]
    attach = attach_ref[...]
    r = iota((1, rows), 1)
    in_tile = (iota((tiles, rows), 0) == (attach >> 7)).astype(jnp.float32).astype(jnp.bfloat16)
    in_lane = iota((LANES, rows), 0) == (attach & (LANES - 1))
    for n, value in enumerate(((r >> 7) + 1, r & (LANES - 1))):
        weighted = jnp.where(in_lane, value.astype(jnp.float32), 0.0).astype(jnp.bfloat16)
        inv_ref[n] = lax.dot_general(in_tile, weighted, NT, preferred_element_type=jnp.float32).astype(jnp.int32)


def image_kernel(pair_ref, attach_ref, stiff_ref, v_ref, p_ref, low_ref, high_ref, p_edge_ref, back_ref, image_ref, inv_ref):
    inverse(attach_ref, inv_ref)
    tiles, chunks = inv_ref.shape[1], back_ref.shape[0] // 4
    at = adjusted(pair_ref, stiff_ref, v_ref, p_ref, (low_ref, high_ref, p_edge_ref))

    def step(i, carry):
        here = pl.ds(pl.multiple_of(i * LANES, LANES), LANES)
        chunk = jnp.broadcast_to(inv_ref[0, pl.ds(i, 1), :], (OCT, LANES))
        index = jnp.broadcast_to(inv_ref[1, pl.ds(i, 1), :], (OCT, LANES))
        _, w_tile = at(i)
        for j, (k2, o) in enumerate(OCTETS):
            back = jnp.zeros((OCT, LANES), jnp.float32)
            for c in range(chunks):
                back = jnp.where(chunk == c + 1, pick(back_ref[4 * c + j], index), back)
            image_ref[k2, o, here] = w_tile[j] + back
        return carry

    lax.fori_loop(0, tiles, step, 0, unroll=8)


def vmem():
    return pl.BlockSpec(memory_space=pltpu.VMEM)


def smem():
    return pl.BlockSpec(memory_space=pltpu.SMEM)


def params(mebibytes):
    return pltpu.CompilerParams(vmem_limit_bytes=mebibytes * 1024 * 1024)


def cost(microseconds):
    return pl.CostEstimate(flops=int(microseconds * 1e9), bytes_accessed=0, transcendentals=0)


HARM, GRP, PLANE = ("y", "z"), ("x", "core"), ("y", "x", "core")


def spread_sum(part, axes):
    count = math.prod(lax.axis_size(axis) for axis in axes)
    return jnp.sum(lax.all_to_all(jnp.broadcast_to(part[None], (count,) + part.shape), axes, 0, 0), axis=0)


def local(vectors, stiffness, attach, live, pair_harm, mistune):
    slot_count, vecs, width = vectors.shape
    rows, blades, tiles = attach.shape[0], 2 * pair_harm.shape[0], width // LANES
    harm_size = lax.axis_size("y") * lax.axis_size("z")
    grp_size = lax.axis_size("x") * lax.axis_size("core")
    block = jax.ShapeDtypeStruct(vectors.shape, jnp.float32)
    packed_rows = jax.ShapeDtypeStruct((4 * harm_size, LANES), jnp.float32)

    half = harm_size // 2
    to_partner = [(i, i ^ half) for i in range(harm_size)]
    partner = lax.ppermute(vectors, HARM, to_partner)
    edge = jax.ShapeDtypeStruct((slot_count, vecs, 1), jnp.float32)
    packed, head, tail = pl.pallas_call(
        gather_kernel,
        out_shape=(
            packed_rows,
            edge,
            edge,
        ),
        in_specs=[pl.BlockSpec(memory_space=pltpu.HBM)] * 2,
        out_specs=(vmem(),) * 3,
        scratch_shapes=[
            pltpu.SMEM(attach.shape, jnp.int32),
            pltpu.VMEM(vectors.shape, jnp.float32),
            pltpu.VMEM((width, 2 * vecs), jnp.float32),
            pltpu.VMEM((rows, 2 * vecs), jnp.float32),
            pltpu.SemaphoreType.DMA((9,)),
        ],
        compiler_params=params(62),
        cost_estimate=cost(5),
        name="gather",
    )(attach, vectors)
    recv = lax.all_to_all(packed.reshape(harm_size, 4, LANES), HARM, 0, 0)
    ends = grp_size - 1
    low_edge = lax.ppermute(tail, GRP, [(i, i + 1) for i in range(ends)])
    high_edge = lax.ppermute(head, GRP, [(i + 1, i) for i in range(ends)])

    basis, coup = pl.pallas_call(
        table_kernel,
        out_shape=(
            jax.ShapeDtypeStruct((blades, blades), jnp.float32),
            jax.ShapeDtypeStruct((2, OCT, LANES), jnp.float32),
        ),
        in_specs=[vmem()],
        out_specs=(vmem(),) * 2,
        compiler_params=params(8),
        cost_estimate=cost(1),
        name="tables",
    )(pair_harm.reshape(1, -1))
    carried = 5 * harm_size
    back = pl.pallas_call(
        blade_kernel,
        out_shape=jax.ShapeDtypeStruct((carried, LANES), jnp.float32),
        in_specs=[vmem()] * 6,
        out_specs=vmem(),
        compiler_params=params(16),
        cost_estimate=cost(1),
        name="blades",
    )(live.reshape(1, 1), recv.reshape(4 * harm_size, LANES), mistune.reshape(-1, LANES), basis, low_edge, high_edge)
    back = lax.all_to_all(back.reshape(carried, 1, LANES), HARM, 0, 0, tiled=True).reshape(carried, LANES)

    stiff = stiffness.reshape(-1, LANES)
    gram, cols = pl.pallas_call(
        adjust_kernel,
        out_shape=(
            jax.ShapeDtypeStruct((2 * vecs, vecs), jnp.float32),
            jax.ShapeDtypeStruct((4 * vecs, rows + LANES), jnp.float32),
        ),
        in_specs=[smem(), smem()] + [vmem()] * 3,
        out_specs=(vmem(),) * 2,
        scratch_shapes=[pltpu.VMEM((width, 4 * vecs), jnp.float32), pltpu.VMEM((rows, 4 * vecs), jnp.float32)],
        compiler_params=params(16),
        cost_estimate=cost(40),
        name="adjust",
    )(pair_harm, attach, stiff, vectors, partner)
    gram, back_tiles, partner_edge = pl.pallas_call(
        functools.partial(cross_kernel, width),
        out_shape=(
            jax.ShapeDtypeStruct((2 * vecs, vecs), jnp.float32),
            jax.ShapeDtypeStruct((4 * rows // LANES, OCT, LANES), jnp.float32),
            jax.ShapeDtypeStruct((slot_count, vecs, 2), jnp.float32),
        ),
        in_specs=[vmem()] * 7,
        out_specs=(vmem(),) * 3,
        compiler_params=params(8),
        cost_estimate=cost(1),
        name="cross",
    )(coup, attach.reshape(1, -1), back, cols, gram, low_edge, high_edge)
    total = spread_sum(gram.reshape(4, LANES), PLANE)
    image = pl.pallas_call(
        image_kernel,
        out_shape=block,
        in_specs=[smem()] + [vmem()] * 8,
        out_specs=vmem(),
        scratch_shapes=[pltpu.VMEM((2, tiles, LANES), jnp.int32)],
        compiler_params=params(8),
        cost_estimate=cost(20),
        name="image",
    )(pair_harm, attach.reshape(1, -1), stiff, vectors, partner, low_edge, high_edge, partner_edge, back_tiles)
    total = spread_sum(total, ("z",))
    return (image, total.reshape(2, vecs, vecs))


def solution(mesh):
    shape = (4, 16, 4, 2)
    mesh = jax.sharding.Mesh(mesh.devices.reshape(shape), ("y", "z", "x", "core"))
    in_specs = (P(HARM, None, GRP), P(GRP), P(GRP), P(GRP), P(), P(None, GRP, None))
    out_specs = (P(HARM, None, GRP), P())
    return jax.shard_map(local, mesh=mesh, in_specs=in_specs, out_specs=out_specs, check_vma=False)
```

```python
import functools
import math

import jax
import jax.numpy as jnp
from jax import lax
from jax.experimental import pallas as pl
from jax.experimental.pallas import tpu as pltpu
from jax.sharding import PartitionSpec as P

LANES = 128
OCT = 8
PIECE = 16


def iota(shape, dim):
    return lax.broadcasted_iota(jnp.int32, shape, dim)


def pick(tile, index):
    return jnp.take_along_axis(tile, index, axis=1, mode="promise_in_bounds")


def swap_blocks(tile):
    sub = iota(tile.shape, 0)
    block = iota(tile.shape, 1) // PIECE
    for bit in (1, 2, 4):
        from_low = pltpu.roll(pltpu.roll(tile, bit, 0), LANES - PIECE * bit, 1)
        from_high = pltpu.roll(pltpu.roll(tile, OCT - bit, 0), PIECE * bit, 1)
        s, b = (sub & bit) != 0, (block & bit) != 0
        tile = jnp.where(s & ~b, from_low, jnp.where(~s & b, from_high, tile))
    return tile


NT = (((1,), (1,)), ((), ()))
TN = (((0,), (0,)), ((), ()))


def dot_f32(a, b, dims):
    return lax.dot_general(a, b, dims, precision=lax.Precision.HIGHEST, preferred_element_type=jnp.float32)


def split(x, parts):
    out = []
    for _ in range(parts):
        out.append(x.astype(jnp.bfloat16))
        x = x - out[-1].astype(jnp.float32)
    return out


def angle_of(harmonic, imag, slots):
    wide = 2.0 * math.pi * harmonic.astype(jnp.float32) / slots
    return jnp.where(harmonic == 0, jnp.where(imag, math.pi, 0.0), wide)


def harm_index():
    return lax.axis_index("y") * lax.axis_size("z") + lax.axis_index("z")


def own_terms(pair_ref, k2):
    half = pair_ref.shape[-1]
    slot = 2 * harm_index() + k2
    if len(pair_ref.shape) == 1:
        harmonic = jnp.full((OCT, LANES), pair_ref[lax.rem(slot, half)], jnp.int32)
    else:
        pairs = jnp.broadcast_to(jnp.concatenate([pair_ref[...]] * 2, axis=1), (OCT, LANES))
        harmonic = pick(pairs, jnp.full((OCT, LANES), lax.rem(slot, half), jnp.int32))
    imag = jnp.full((OCT, LANES), slot, jnp.int32) >= half
    theta = angle_of(harmonic, imag, 2 * half)
    coup = jnp.where(harmonic == 0, 0.0, jnp.where(imag, -1.0, 1.0) * jnp.sin(theta))
    return 2.0 + 2.0 * (1.0 - jnp.cos(theta)), coup


OCTETS = [(j // 2, slice(OCT * (j % 2), OCT * (j % 2) + OCT)) for j in range(4)]


def fetch(attach_ref, t_ref, g_ref):
    group = 64

    def step(n, carry):
        for u in range(group):
            at = attach_ref[n * group + u]
            g_ref[pl.ds(pl.multiple_of(n * group, group) + u, 1), :] = t_ref[pl.ds(at, 1), :]
        return carry

    lax.fori_loop(0, attach_ref.shape[0] // group, step, 0)


def gather_kernel(attach_hbm, v_hbm, out_ref, head_ref, tail_ref, attach_ref, v_ref, t_ref, g_ref, sems):
    parts, width = sems.shape[0] - 1, v_ref.shape[2]
    span = width // parts
    copies = [
        pltpu.make_async_copy(v_hbm.at[:, :, pl.ds(n * span, span)], v_ref.at[:, :, pl.ds(n * span, span)], sems.at[n])
        for n in range(parts)
    ]
    table = pltpu.make_async_copy(attach_hbm, attach_ref, sems.at[parts])
    for copy in copies[:1] + [table] + copies[1:]:
        copy.start()
    for n, copy in enumerate(copies):
        copy.wait()
        for i in range(n * span // LANES, (n + 1) * span // LANES):
            here = slice(LANES * i, LANES * (i + 1))
            t_ref[here, :] = jnp.concatenate([v_ref[k2, o, here] for k2, o in OCTETS], axis=0).T
    head_ref[...] = v_ref[:, :, :1]
    tail_ref[...] = v_ref[:, :, width - 1 :]
    table.wait()
    fetch(attach_ref, t_ref, g_ref)
    owners = out_ref.shape[0] // 4
    part = iota((owners, LANES), 1) // 32
    for m in range(4):
        out = None
        for b in range(4):
            x = jnp.concatenate([g_ref[pl.ds(4 * b + m, owners, stride=PIECE), :]] * 4, axis=1)
            out = x if out is None else jnp.where(part == b, x, out)
        out_ref[pl.ds(m, owners, stride=4), :] = out


def table_kernel(pair_ref, mistune_ref, basis_ref, coup_ref, stiff_ref):
    me, blades = harm_index(), basis_ref.shape[0]
    chunk = mistune_ref[pl.ds(me // OCT, blades, stride=OCT), :]
    index = lax.rem(me, OCT) * PIECE + iota((blades, LANES), 1) // PIECE
    stiff_ref[:, :LANES] = pick(chunk, index)
    stiff_ref[:, LANES:] = pick(chunk, index + OCT)
    for k2 in range(2):
        coup_ref[k2] = own_terms(pair_ref, k2)[1]
    half = pair_ref.shape[1]
    slots = 2 * half
    pairs = jnp.broadcast_to(jnp.concatenate([pair_ref[...]] * 2, axis=1), (OCT, slots))
    lane = iota((OCT, slots), 1)
    slot = 2 * (lane & (half - 1)) + lane // half
    harmonic = pick(pairs, slot & (half - 1))
    imag = slot >= half
    theta = angle_of(harmonic, imag, slots)
    for n in range(slots // OCT):
        angle = (iota((OCT, slots), 0) + OCT * n).astype(jnp.float32) * theta
        cosine = jnp.cos(angle)
        wide = math.sqrt(2.0 / slots) * jnp.where(imag, jnp.sin(angle), cosine)
        basis_ref[OCT * n : OCT * (n + 1), :] = jnp.where(harmonic == 0, cosine / math.sqrt(slots), wide)


def shifted(ref, k2, o, i, count, low, high):
    here = pl.ds(pl.multiple_of(i * LANES, LANES), LANES)
    after = pl.ds(pl.multiple_of(jnp.minimum(i + 1, count - 1) * LANES, LANES), LANES)
    before = pl.ds(pl.multiple_of(jnp.maximum(i - 1, 0) * LANES, LANES), LANES)
    lane = iota((OCT, LANES), 1)
    v = ref[k2, o, here]
    prev = jnp.where(i == 0, low, ref[k2, o, before])
    follow = jnp.where(i == count - 1, high, ref[k2, o, after])
    lo = pltpu.roll(jnp.where(lane == LANES - 1, prev, v), 1, 1)
    hi = pltpu.roll(jnp.where(lane == 0, follow, v), LANES - 1, 1)
    return v, lo, hi


def adjusted(pair_ref, stiff_ref, v_ref, p_ref, edge_refs):
    tiles = stiff_ref.shape[0]
    terms = [own_terms(pair_ref, k2) for k2 in range(2)]
    if edge_refs is None:
        low = high = p_low = p_high = [jnp.zeros((OCT, LANES), jnp.float32)] * 4
    else:
        low, high = [[jnp.broadcast_to(ref[k2, o, :], (OCT, LANES)) for k2, o in OCTETS] for ref in edge_refs[:2]]
        p_low, p_high = [[jnp.broadcast_to(edge_refs[2][k2, o, n : n + 1], (OCT, LANES)) for k2, o in OCTETS] for n in range(2)]

    def at(i):
        stiff = jnp.broadcast_to(stiff_ref[pl.ds(i, 1), :], (OCT, LANES))
        v_tile, w_tile = [], []
        for j, (k2, o) in enumerate(OCTETS):
            v, lo, hi = shifted(v_ref, k2, o, i, tiles, low[j], high[j])
            _, p_lo, p_hi = shifted(p_ref, k2, o, i, tiles, p_low[j], p_high[j])
            v_tile.append(v)
            w_tile.append((terms[k2][0] + stiff) * v - lo - hi + terms[k2][1] * (p_hi - p_lo))
        return v_tile, w_tile

    return at


def adjust_kernel(pair_ref, attach_ref, stiff_ref, v_ref, p_ref, gram_ref, cols_ref, t_ref, g_ref):
    tiles, vecs, per = stiff_ref.shape[0], v_ref.shape[1], 8
    at = adjusted(pair_ref, stiff_ref, v_ref, p_ref, None)

    def step(g, gram):
        vs, ws = [], []
        for t in range(per):
            i = g * per + t
            v_tile, w_tile = at(i)
            here = pl.ds(pl.multiple_of(i * LANES, LANES), LANES)
            t_ref[here, :] = jnp.concatenate(v_tile + w_tile, axis=0).T
            vs.append(jnp.concatenate(v_tile, axis=0))
            ws.append(jnp.concatenate(w_tile, axis=0))
        v, w = jnp.concatenate(vs, axis=1), jnp.concatenate(ws, axis=1)
        for k2 in range(2):
            own = slice(vecs * k2, vecs * (k2 + 1))
            w3 = split(w[own], 3)
            left = jnp.concatenate(split(v[own], 3) + w3, axis=0)
            gram = gram + lax.dot_general(left, jnp.concatenate(w3, axis=0), NT, preferred_element_type=jnp.float32)
        return gram

    total = lax.fori_loop(0, tiles // per, step, jnp.zeros((6 * vecs, 3 * vecs), jnp.float32))
    for n in range(2):
        gram = jnp.zeros((vecs, vecs), jnp.float32)
        for a in range(3):
            for b in range(3 - a):
                at = (3 * n + a) * vecs
                gram = gram + total[at : at + vecs, b * vecs : (b + 1) * vecs]
        gram_ref[n * vecs : (n + 1) * vecs, :] = gram
    fetch(attach_ref, t_ref, g_ref)
    rows, last = g_ref.shape[0], t_ref.shape[0] - 1
    for c in range(rows // LANES):
        here = slice(LANES * c, LANES * (c + 1))
        cols_ref[:, here] = g_ref[here, :].T
    g_ref[:LANES, :] = jnp.zeros((LANES, g_ref.shape[1]), jnp.float32)
    g_ref[0:1, :] = t_ref[0:1, :]
    g_ref[1:2, :] = t_ref[last : last + 1, :]
    cols_ref[:, rows:] = g_ref[:LANES, :].T


def blade_kernel(live_ref, recv_ref, stiff_ref, basis_ref, out_ref, zero_ref):
    zero_ref[...] = jnp.zeros(zero_ref.shape, jnp.float32)
    me, live = harm_index(), live_ref[...]
    owners = out_ref.shape[0] // 4
    blades = 2 * owners
    slab = [recv_ref[pl.ds(m, owners, stride=4), :] for m in range(4)]
    piece = iota((owners, LANES), 1) // PIECE

    def arrived(k2):
        halves = []
        for half in range(2):
            out = None
            for n in range(OCT):
                r = OCT * half + n
                at = 2 * (r // 4) + k2
                tile = slab[r % 4] if at == n else pltpu.roll(slab[r % 4], (PIECE * (n - at)) % LANES, 1)
                out = tile if out is None else jnp.where(piece == n, tile, out)
            halves.append(out)
        return jnp.concatenate(halves, axis=1)

    wide = 2 * LANES
    alive = me * PIECE + iota((1, wide), 1) // PIECE < live
    rows = jnp.where(alive, jnp.concatenate([arrived(0), arrived(1)], axis=0), 0.0)
    mm = (((1,), (0,)), ((), ()))
    blade = dot_f32(basis_ref[...], rows, mm)
    back = jnp.where(alive, dot_f32(basis_ref[...], stiff_ref[...] * blade, TN), 0.0)
    down, across = iota((wide, wide), 0), iota((wide, wide), 1)
    swap = ((down & (PIECE - 1)) == across // PIECE) & (down // PIECE == (across & (PIECE - 1)))
    parts = jnp.concatenate(split(back, 3), axis=0)
    parts = jnp.dot(parts, swap.astype(jnp.float32).astype(jnp.bfloat16), preferred_element_type=jnp.float32)
    turned = parts[:blades] + parts[blades : 2 * blades] + parts[2 * blades :]
    for j in range(4):
        k2, vh = j // 2, j % 2
        out_ref[pl.ds(j, owners, stride=4), :] = turned[owners * k2 : owners * (k2 + 1), LANES * vh : LANES * (vh + 1)]


def cross_kernel(width, coup_ref, attach_ref, recv_ref, cols_ref, gram_ref, low_ref, high_ref, p_edge_ref, total_ref, back_ref):
    vecs, rows = gram_ref.shape[1], attach_ref.shape[1]
    chunks = rows // LANES
    tiles = [[swap_blocks(recv_ref[pl.ds(4 * OCT * c + j, OCT, stride=4), :]) for c in range(chunks)] for j in range(4)]
    attach = attach_ref[...]
    at_first, at_last = attach == 0, attach == width - 1
    lane = iota((vecs, LANES), 1)
    for k2 in range(2):
        coup = coup_ref[k2, 0:1, 0:1]
        both = []
        for j in (2 * k2, 2 * k2 + 1):
            for c in range(chunks):
                back_ref[4 * c + j] = tiles[j][c]
            both.append(jnp.concatenate(tiles[j], axis=1))
        back = jnp.concatenate(both, axis=0)
        first = -low_ref[k2] - coup * p_edge_ref[k2, :, 0:1]
        last = -high_ref[k2] + coup * p_edge_ref[k2, :, 1:2]
        outer = jnp.where(lane == 0, first, jnp.where(lane == 1, last, 0.0))
        at_rows = jnp.where(at_first, first, jnp.where(at_last, last, 0.0))
        more = jnp.concatenate([back, outer], axis=1)
        adj = cols_ref[vecs * (k2 + 2) : vecs * (k2 + 3), :] + jnp.concatenate([at_rows, jnp.zeros_like(outer)], axis=1)
        left = jnp.concatenate([cols_ref[vecs * k2 : vecs * (k2 + 1), :], adj + 0.5 * more], axis=0)
        term = dot_f32(left, more, NT)
        terms = term if k2 == 0 else terms + term
    unit = (iota((vecs, vecs), 0) == iota((vecs, vecs), 1)).astype(jnp.float32)
    twice = dot_f32(unit, terms[vecs:], NT)
    total_ref[...] = gram_ref[...] + terms + jnp.concatenate([jnp.zeros_like(twice), twice], axis=0)


def inverse(attach_ref, inv_ref):
    tiles, rows = inv_ref.shape[1], attach_ref.shape[1]
    attach = attach_ref[...]
    r = iota((1, rows), 1)
    in_tile = (iota((tiles, rows), 0) == (attach >> 7)).astype(jnp.float32).astype(jnp.bfloat16)
    in_lane = iota((LANES, rows), 0) == (attach & (LANES - 1))
    for n, value in enumerate(((r >> 7) + 1, r & (LANES - 1))):
        weighted = jnp.where(in_lane, value.astype(jnp.float32), 0.0).astype(jnp.bfloat16)
        inv_ref[n] = lax.dot_general(in_tile, weighted, NT, preferred_element_type=jnp.float32).astype(jnp.int32)


def image_kernel(pair_ref, attach_ref, stiff_ref, v_ref, p_ref, low_ref, high_ref, p_edge_ref, back_ref, image_ref, inv_ref):
    inverse(attach_ref, inv_ref)
    tiles, chunks = inv_ref.shape[1], back_ref.shape[0] // 4
    at = adjusted(pair_ref, stiff_ref, v_ref, p_ref, (low_ref, high_ref, p_edge_ref))

    def step(i, carry):
        here = pl.ds(pl.multiple_of(i * LANES, LANES), LANES)
        chunk = jnp.broadcast_to(inv_ref[0, pl.ds(i, 1), :], (OCT, LANES))
        index = jnp.broadcast_to(inv_ref[1, pl.ds(i, 1), :], (OCT, LANES))
        _, w_tile = at(i)
        for j, (k2, o) in enumerate(OCTETS):
            back = jnp.zeros((OCT, LANES), jnp.float32)
            for c in range(chunks):
                back = jnp.where(chunk == c + 1, pick(back_ref[4 * c + j], index), back)
            image_ref[k2, o, here] = w_tile[j] + back
        return carry

    lax.fori_loop(0, tiles, step, 0, unroll=8)


def vmem():
    return pl.BlockSpec(memory_space=pltpu.VMEM)


def smem():
    return pl.BlockSpec(memory_space=pltpu.SMEM)


def params(mebibytes):
    return pltpu.CompilerParams(vmem_limit_bytes=mebibytes * 1024 * 1024)


def cost(microseconds):
    return pl.CostEstimate(flops=int(microseconds * 1e9), bytes_accessed=0, transcendentals=0)


HARM, GRP, PLANE = ("y", "z"), ("x", "core"), ("y", "x", "core")


def spread_sum(part, axes):
    count = math.prod(lax.axis_size(axis) for axis in axes)
    return jnp.sum(lax.all_to_all(jnp.broadcast_to(part[None], (count,) + part.shape), axes, 0, 0), axis=0)


def local(vectors, stiffness, attach, live, pair_harm, mistune):
    slot_count, vecs, width = vectors.shape
    rows, blades, tiles = attach.shape[0], 2 * pair_harm.shape[0], width // LANES
    harm_size = lax.axis_size("y") * lax.axis_size("z")
    grp_size = lax.axis_size("x") * lax.axis_size("core")
    block = jax.ShapeDtypeStruct(vectors.shape, jnp.float32)
    packed_rows = jax.ShapeDtypeStruct((4 * harm_size, LANES), jnp.float32)

    half = harm_size // 2
    to_partner = [(i, i ^ half) for i in range(harm_size)]
    partner = lax.ppermute(vectors, HARM, to_partner)
    edge = jax.ShapeDtypeStruct((slot_count, vecs, 1), jnp.float32)
    packed, head, tail = pl.pallas_call(
        gather_kernel,
        out_shape=(
            packed_rows,
            edge,
            edge,
        ),
        in_specs=[pl.BlockSpec(memory_space=pltpu.HBM)] * 2,
        out_specs=(vmem(),) * 3,
        scratch_shapes=[
            pltpu.SMEM(attach.shape, jnp.int32),
            pltpu.VMEM(vectors.shape, jnp.float32),
            pltpu.VMEM((width, 2 * vecs), jnp.float32),
            pltpu.VMEM((rows, 2 * vecs), jnp.float32),
            pltpu.SemaphoreType.DMA((9,)),
        ],
        compiler_params=params(62),
        cost_estimate=cost(5),
        name="gather",
    )(attach, vectors)
    recv = lax.all_to_all(packed.reshape(harm_size, 4, LANES), HARM, 0, 0)
    ends = grp_size - 1
    low_edge = lax.ppermute(tail, GRP, [(i, i + 1) for i in range(ends)])
    high_edge = lax.ppermute(head, GRP, [(i + 1, i) for i in range(ends)])

    basis, coup, stiff_rows = pl.pallas_call(
        table_kernel,
        out_shape=(
            jax.ShapeDtypeStruct((blades, blades), jnp.float32),
            jax.ShapeDtypeStruct((2, OCT, LANES), jnp.float32),
            jax.ShapeDtypeStruct((blades, 2 * LANES), jnp.float32),
        ),
        in_specs=[vmem()] * 2,
        out_specs=(vmem(),) * 3,
        compiler_params=params(8),
        cost_estimate=cost(1),
        name="tables",
    )(pair_harm.reshape(1, -1), mistune.reshape(-1, LANES))
    back, zero = pl.pallas_call(
        blade_kernel,
        out_shape=(packed_rows, jax.ShapeDtypeStruct((slot_count, vecs, 2), jnp.float32)),
        in_specs=[vmem()] * 4,
        out_specs=(vmem(),) * 2,
        compiler_params=params(16),
        cost_estimate=cost(1),
        name="blades",
    )(live.reshape(1, 1), recv.reshape(4 * harm_size, LANES), stiff_rows, basis)
    back = lax.all_to_all(back.reshape(harm_size, 4, LANES), HARM, 0, 0)
    partner_edge = lax.ppermute(jnp.concatenate([low_edge, high_edge], axis=2) + zero, HARM, to_partner)

    stiff = stiffness.reshape(-1, LANES)
    gram, cols = pl.pallas_call(
        adjust_kernel,
        out_shape=(
            jax.ShapeDtypeStruct((2 * vecs, vecs), jnp.float32),
            jax.ShapeDtypeStruct((4 * vecs, rows + LANES), jnp.float32),
        ),
        in_specs=[smem(), smem()] + [vmem()] * 3,
        out_specs=(vmem(),) * 2,
        scratch_shapes=[pltpu.VMEM((width, 4 * vecs), jnp.float32), pltpu.VMEM((rows, 4 * vecs), jnp.float32)],
        compiler_params=params(16),
        cost_estimate=cost(40),
        name="adjust",
    )(pair_harm, attach, stiff, vectors, partner)
    gram, back_tiles = pl.pallas_call(
        functools.partial(cross_kernel, width),
        out_shape=(
            jax.ShapeDtypeStruct((2 * vecs, vecs), jnp.float32),
            jax.ShapeDtypeStruct((4 * rows // LANES, OCT, LANES), jnp.float32),
        ),
        in_specs=[vmem()] * 8,
        out_specs=(vmem(),) * 2,
        compiler_params=params(8),
        cost_estimate=cost(1),
        name="cross",
    )(coup, attach.reshape(1, -1), back.reshape(4 * harm_size, LANES), cols, gram, low_edge, high_edge, partner_edge)
    total = spread_sum(gram.reshape(4, LANES), PLANE)
    image = pl.pallas_call(
        image_kernel,
        out_shape=block,
        in_specs=[smem()] + [vmem()] * 8,
        out_specs=vmem(),
        scratch_shapes=[pltpu.VMEM((2, tiles, LANES), jnp.int32)],
        compiler_params=params(8),
        cost_estimate=cost(20),
        name="image",
    )(pair_harm, attach.reshape(1, -1), stiff, vectors, partner, low_edge, high_edge, partner_edge, back_tiles)
    total = spread_sum(total, ("z",))
    return (image, total.reshape(2, vecs, vecs))


def solution(mesh):
    shape = (4, 16, 4, 2)
    mesh = jax.sharding.Mesh(mesh.devices.reshape(shape), ("y", "z", "x", "core"))
    in_specs = (P(HARM, None, GRP), P(GRP), P(GRP), P(GRP), P(), P(None, GRP, None))
    out_specs = (P(HARM, None, GRP), P())
    return jax.shard_map(local, mesh=mesh, in_specs=in_specs, out_specs=out_specs, check_vma=False)
```
